128 devices in a mesh: row: 4 (over y), col: 32 (over z, x, core).
Axes of the slice: x: 4, y: 4, z: 4, core: 2. Of those that a mesh axis runs over, the one named last changes fastest.
Arguments:
- amplitudes: bfloat16 [8192, 4096], P('row', 'col'), may hold values from -6 to 6
- integrals: bfloat16 [4096, 32768], P('row', 'col'), may hold values from -0.09375 to 0.09375
- amp_mask: int32 [128, 64], replicated, may hold values 0 or 1
- int_mask: int32 [64, 512], replicated, may hold values 0 or 1
- pair_map: int32 [128], replicated, may hold values from 0 to 127, each once
Outputs:
- ladder: bfloat16 [8192, 32768], P('row', 'col')
The draws below stay inside these ranges and needn't reach their ends.
All inputs are finite; a program needn't handle non-finite values.
Results may differ from the reference program's by a relative error of at most 0.0015.
Values may be sent and summed in bfloat16 or wider, within the bound.
A program may use at most 128 MiB of HBM per device.

```python
import jax
import jax.numpy as jnp
from jax import lax

TILE = 64
PT = 128
ROWS = 8192
KTILES = 64
KDIM = 4096
NTILES = 512
NDIM = 32768
N_COL = 32


def place_ends(result, own_key, smallest, top_value):
    longest = result.shape.index(max(result.shape))
    spots = []
    for shift in (0, 1):
        where = [jax.random.randint(jax.random.fold_in(own_key, axis), (), 0, length) for axis, length in enumerate(result.shape)]
        where[longest] = (where[longest] + shift) % result.shape[longest]
        spots.append(tuple(where))
    return result.at[spots[0]].set(smallest).at[spots[1]].set(top_value)


def block_levels(own_key, dims, split, smallest, high):
    gain, own = 1.0, jax.random.fold_in(own_key, 6)
    for dim, shards_of in split:
        draws = jnp.exp(jax.random.uniform(jax.random.fold_in(own, dim), (shards_of,), jnp.float32, smallest / len(split), high / len(split)))
        gain = gain * jnp.repeat(draws, dims[dim] // shards_of).reshape([-1 if axis == dim else 1 for axis in range(len(dims))])
    return gain


def bell_draw(rng, dims, deviation, bound, shards=(), kind=jnp.bfloat16):
    array = jax.random.normal(rng, dims, jnp.float32) * deviation
    if len(shards) > 0:
        array = block_levels(rng, dims, shards, -0.22, 0.18) * array
    return jnp.clip(array, min=-bound, max=bound).astype(kind)


def setup_inputs(seed: int = 0) -> dict:
    seeds = jax.random.split(jax.random.key(seed), 6)
    return {
        "amplitudes": bell_draw(seeds[0], (ROWS, KDIM), 1.0, 6.0, ((0, 4), (1, 32))),
        "integrals": bell_draw(seeds[1], (KDIM, NDIM), KDIM ** -0.5, 0.09375, ((0, 4), (1, 32))),
        "amp_mask": place_ends((jax.random.randint(seeds[2], (PT, KTILES), 0, 20) < 19).astype(jnp.int32), jax.random.fold_in(seeds[2], 1), 0, 1),
        "int_mask": place_ends((jax.random.randint(seeds[3], (KTILES, NTILES), 0, 20) < 19).astype(jnp.int32), jax.random.fold_in(seeds[3], 1), 0, 1),
        "pair_map": jax.random.permutation(seeds[4], PT).astype(jnp.int32),
    }


def spread(tile_flags):
    wide = jnp.repeat(jnp.repeat(tile_flags, TILE, 0), TILE, 1)
    return wide.astype(jnp.bfloat16)


def reference(amplitudes, integrals, amp_mask, int_mask, pair_map):
    masked_amp = amplitudes * spread(amp_mask)
    masked_int = integrals * spread(int_mask)
    slab_cols = NDIM // N_COL
    stacked = masked_int.reshape(KDIM, N_COL, slab_cols).transpose(1, 0, 2)

    def multiply(column_slab):
        return jnp.dot(masked_amp, column_slab, preferred_element_type=jnp.float32).astype(jnp.bfloat16)

    blocks = lax.map(multiply, stacked)
    product = blocks.transpose(1, 0, 2).reshape(ROWS, NDIM)
    tiled = product.reshape(PT, TILE, NDIM)
    return tiled[pair_map.astype(jnp.int32)].reshape(ROWS, NDIM)
```

```python
import jax
import jax.numpy as jnp
from jax import lax
from jax.sharding import PartitionSpec as P

TILE = 64


def spread(tile_flags):
    wide = jnp.repeat(jnp.repeat(tile_flags, TILE, 0), TILE, 1)
    return wide.astype(jnp.bfloat16)


def local(amplitudes, integrals, amp_mask, int_mask, pair_map):
    row_index = lax.axis_index("row")
    col_index = lax.axis_index("col")
    rows_here, amp_cols = amplitudes.shape
    row_tiles = rows_here // TILE
    amp_ktiles = amp_cols // TILE
    chosen = lax.dynamic_slice_in_dim(pair_map, row_index * row_tiles, row_tiles, 0)
    int_rows, out_cols = integrals.shape
    int_ktiles = int_rows // TILE
    out_tiles = out_cols // TILE
    int_flags = lax.dynamic_slice(
        int_mask, (row_index * int_ktiles, col_index * out_tiles), (int_ktiles, out_tiles)
    )
    masked_int = integrals * spread(int_flags)
    every_amp = lax.all_gather(amplitudes, "row", axis=0, tiled=True)
    picked = every_amp.reshape(-1, TILE, amp_cols)[chosen].reshape(rows_here, amp_cols)
    flag_cols = lax.dynamic_slice_in_dim(amp_mask, col_index * amp_ktiles, amp_ktiles, 1)
    masked_amp = picked * spread(flag_cols[chosen])
    full_amp = lax.all_gather(masked_amp, "col", axis=1, tiled=True)
    full_int = lax.all_gather(masked_int, "row", axis=0, tiled=True)
    summed = jnp.dot(full_amp, full_int, preferred_element_type=jnp.float32)
    return summed.astype(jnp.bfloat16)


def solution(mesh):
    in_specs = (P("row", "col"), P("row", "col"), P(), P(), P())
    out_specs = P("row", "col")
    return jax.shard_map(local, mesh=mesh, in_specs=in_specs, out_specs=out_specs, check_vma=False)
```

```python
import jax
import jax.numpy as jnp
from jax import lax
from jax.experimental import pallas as pl
from jax.experimental.pallas import tpu as pltpu
from jax.sharding import PartitionSpec as P

TILE = 64
MESH = pl.DeviceIdType.MESH
CHUNKS = 4
WIDE = 256
ROWS_STEP = 512


class Ring:
    def __init__(self, slot, down, up, send, recv, own=None):
        own = own or (lambda half: slot(0, half))
        routes = (
            (own(0), slot(0, 0), up),
            (own(1), slot(0, 1), down),
            (own(1), slot(0, 1), up),
            (own(0), slot(0, 0), down),
            (slot(-1, 0), slot(-1, 0), up),
            (slot(1, 1), slot(1, 1), down),
        )
        self.copies = [
            pltpu.make_async_remote_copy(
                src_ref=src, dst_ref=dst, send_sem=send.at[i], recv_sem=recv.at[i], device_id=to, device_id_type=MESH
            )
            for i, (src, dst, to) in enumerate(routes)
        ]

    def start(self):
        for copy in self.copies[:4]:
            copy.start()

    def forward(self):
        for i in (0, 1):
            self.copies[i].wait_recv()
            self.copies[4 + i].start()

    def near(self):
        for copy in self.copies[2:4]:
            copy.wait_recv()

    def far(self):
        for copy in self.copies[4:]:
            copy.wait_recv()

    def finish(self):
        for copy in self.copies:
            copy.wait_send()


def kernel(
    amp_mask, pair_map, int_mask, amp, ints, out,
    amp_all, full, ints_in, flag_rows, ints_all, stage, total,
    ring_send, ring_recv, relay_send, relay_recv, local_sem, out_sem,
):
    y = lax.axis_index("row")
    col = lax.axis_index("col")
    core = lax.rem(col, 2)
    x = lax.rem(lax.div(col, 2), 4)
    z = lax.div(col, 8)

    def turn(a, d):
        return lax.rem(a + (d + 4), 4)

    def place(dx, dz, c):
        return turn(z, dz) * 8 + turn(x, dx) * 2 + c

    up_y, down_y = (turn(y, 1), col), (turn(y, -1), col)
    up_x, down_x = (y, place(1, 0, core)), (y, place(-1, 0, core))
    up_z, down_z = (y, place(0, 1, core)), (y, place(0, -1, core))
    twin = (y, place(0, 0, 1 - core))

    amp_in = pltpu.make_async_copy(amp, amp_all.at[pl.ds(y * 32, 32)], local_sem.at[0])
    ints_copy = pltpu.make_async_copy(ints, ints_in, local_sem.at[1])
    ints_copy.start()
    amp_in.start()

    barrier = pltpu.get_barrier_semaphore()
    for other in (up_y, down_y, up_x, down_x, up_z, down_z, twin):
        pl.semaphore_signal(barrier, inc=1, device_id=other, device_id_type=MESH)
    pl.semaphore_wait(barrier, 7)

    used = [0]

    def ring(slot, down, up, own=None):
        n = used[0]
        used[0] += 1
        return Ring(slot, down, up, ring_send.at[n], ring_recv.at[n], own)

    ring_a = ring(
        lambda d, half: amp_all.at[pl.ds(turn(y, d) * 32 + half * 16, 16)],
        down_y, up_y, lambda half: amp.at[pl.ds(half * 16, 16)],
    )
    ring_a.start()

    wide = CHUNKS * WIDE
    chosen = lax.broadcasted_iota(jnp.int32, (512, wide), 0)
    lane_tile = lax.broadcasted_iota(jnp.int32, (512, wide), 1) >> 6
    pick = jnp.where(chosen == lane_tile + col * 16, 1.0, 0.0).astype(jnp.bfloat16)
    flags = int_mask[pl.ds(pl.multiple_of(y * 16, 16), 16), :].astype(jnp.float32).astype(jnp.bfloat16)
    flag_rows[...] = jnp.dot(flags, pick, preferred_element_type=jnp.float32)
    ints_copy.wait()
    for j in range(CHUNKS):
        for t in range(16):
            flag = flag_rows[t : t + 1, j * WIDE : (j + 1) * WIDE]
            spread = jnp.broadcast_to(flag, (TILE, WIDE)).astype(jnp.bfloat16)
            block = ints_in[t * TILE : (t + 1) * TILE, j * WIDE : (j + 1) * WIDE]
            ints_all[j, pl.ds(pl.multiple_of(y * 1024 + t * TILE, TILE), TILE), :] = block * spread

    def ring_of_chunk(j):
        return ring(
            lambda d, half: ints_all.at[j, pl.ds(pl.multiple_of(turn(y, d) * 1024 + half * 512, 512), 512)],
            down_y, up_y,
        )

    ring_b = [ring_of_chunk(j) for j in range(CHUNKS)]

    ring_a.forward()
    ring_a.near()
    ring_b[0].start()
    amp_in.wait()
    ring_a.far()

    lane = lax.broadcasted_iota(jnp.int32, (TILE, 128), 1)

    def choose(q, carry):
        tile = pair_map[y * 32 + q]
        left = amp_mask[tile, col * 2]
        right = amp_mask[tile, col * 2 + 1]
        flag = jnp.where(lane < TILE, left, right).astype(jnp.float32).astype(jnp.bfloat16)
        full[col, pl.ds(pl.multiple_of(q * TILE, TILE), TILE), :] = amp_all[tile] * flag
        return carry

    lax.fori_loop(0, 32, choose, 0)

    relays = []

    def relay(dx, dz, start, size):
        n = len(relays)
        piece = full.at[place(dx, dz, core), pl.ds(start, size)]
        copy = pltpu.make_async_remote_copy(
            src_ref=piece, dst_ref=piece, send_sem=relay_send.at[n], recv_sem=relay_recv.at[n],
            device_id=twin, device_id_type=MESH,
        )
        copy.start()
        relays.append(copy)

    def rows_of(part, half):
        return pl.ds(part * 1024 + half * 512, 512)

    def ring_x(part, dz):
        return ring(lambda d, half: full.at[place(d, dz, core), rows_of(part, half)], down_x, up_x)

    def ring_z(part, dx):
        return ring(lambda d, half: full.at[place(dx, d, core), rows_of(part, half)], down_z, up_z)

    first_x, first_z = ring_x(0, 0), ring_z(1, 0)
    then_z = {d: ring_z(0, d) for d in (0, -1, 1, 2)}
    then_x = {d: ring_x(1, d) for d in (0, -1, 1, 2)}
    first_x.start()
    first_z.start()
    relay(0, 0, 0, 2048)
    then_z[0].start()
    then_x[0].start()
    first_x.forward()
    first_z.forward()
    ring_b[0].forward()
    ring_b[1].start()
    first_x.near()
    first_z.near()
    for d in (-1, 1):
        then_z[d].start()
        then_x[d].start()
        relay(d, 0, 0, 1024)
        relay(0, d, 1024, 1024)
    first_x.far()
    first_z.far()
    then_z[2].start()
    then_x[2].start()
    relay(2, 0, 0, 1024)
    relay(0, 2, 1024, 1024)
    for d in (0, -1, 1, 2):
        then_z[d].forward()
        then_x[d].forward()
        then_z[d].near()
        then_x[d].near()
        for e in (-1, 1):
            relay(d, e, 0, 1024)
            relay(e, d, 1024, 1024)
        if d == -1:
            ring_b[1].forward()
            ring_b[2].start()
    for d in (0, -1, 1, 2):
        then_z[d].far()
        then_x[d].far()
        relay(d, 2, 0, 1024)
        relay(2, d, 1024, 1024)
    ring_b[2].forward()
    ring_b[3].start()
    for copy in relays:
        copy.wait_recv()

    def result(j):
        return pltpu.make_async_copy(
            stage.at[j % 2], out.at[:, pl.ds(j * WIDE, WIDE)], out_sem.at[j]
        )

    def lines(m):
        return pl.ds(pl.multiple_of(m * ROWS_STEP, ROWS_STEP), ROWS_STEP)

    def whole(j):
        def step(m, carry):
            left = jnp.concatenate([full[s, lines(m), :] for s in range(32)], axis=1)
            stage[j % 2, lines(m), :] = jnp.dot(
                left, ints_all[j], preferred_element_type=jnp.float32
            ).astype(jnp.bfloat16)
            return carry

        lax.fori_loop(0, 2048 // ROWS_STEP, step, 0)
        result(j).start()

    def part(j, d, m):
        plane = turn(y, d)
        left = jnp.concatenate([full[plane * 8 + s, lines(m), :] for s in range(8)], axis=1)
        right = ints_all[j, pl.ds(pl.multiple_of(plane * 1024, 1024), 1024), :]
        return jnp.dot(left, right, preferred_element_type=jnp.float32)

    def over_rows(body):
        def step(m, carry):
            body(m)
            return carry

        lax.fori_loop(0, 2048 // ROWS_STEP, step, 0)

    ring_b[0].near()
    ring_b[0].far()
    whole(0)
    ring_b[1].near()
    ring_b[1].far()
    whole(1)
    ring_b[3].forward()
    ring_b[2].near()
    ring_b[2].far()
    result(0).wait()
    whole(2)

    last = CHUNKS - 1

    def begin(m):
        total[lines(m), :] = part(last, 0, m)

    def add(d):
        def body(m):
            total[lines(m), :] += part(last, d, m)

        return body

    def end(m):
        stage[last % 2, lines(m), :] = (total[lines(m), :] + part(last, 2, m)).astype(jnp.bfloat16)

    over_rows(begin)
    ring_b[3].near()
    over_rows(add(-1))
    over_rows(add(1))
    result(1).wait()
    ring_b[3].far()
    over_rows(end)
    result(last).start()

    for each in (ring_a, *ring_b, first_x, first_z, *then_z.values(), *then_x.values()):
        each.finish()
    for copy in relays:
        copy.wait_send()
    result(2).wait()
    result(last).wait()


def local(amplitudes, integrals, amp_mask, int_mask, pair_map):
    rings = 15
    relays = 31
    anywhere = pl.BlockSpec(memory_space=pl.ANY)
    return pl.pallas_call(
        kernel,
        out_shape=jax.ShapeDtypeStruct((2048, 1024), jnp.bfloat16),
        in_specs=[
            pl.BlockSpec(memory_space=pltpu.SMEM),
            pl.BlockSpec(memory_space=pltpu.SMEM),
            pl.BlockSpec(memory_space=pltpu.VMEM),
            anywhere,
            anywhere,
        ],
        out_specs=anywhere,
        scratch_shapes=[
            pltpu.VMEM((128, TILE, 128), jnp.bfloat16),
            pltpu.VMEM((32, 2048, 128), jnp.bfloat16),
            pltpu.VMEM((1024, 1024), jnp.bfloat16),
            pltpu.VMEM((16, 1024), jnp.float32),
            pltpu.VMEM((CHUNKS, 4096, WIDE), jnp.bfloat16),
            pltpu.VMEM((2, 2048, WIDE), jnp.bfloat16),
            pltpu.VMEM((2048, WIDE), jnp.float32),
            pltpu.SemaphoreType.DMA((rings, 6)),
            pltpu.SemaphoreType.DMA((rings, 6)),
            pltpu.SemaphoreType.DMA((relays,)),
            pltpu.SemaphoreType.DMA((relays,)),
            pltpu.SemaphoreType.DMA((2,)),
            pltpu.SemaphoreType.DMA((CHUNKS,)),
        ],
        compiler_params=pltpu.CompilerParams(
            collective_id=0, has_side_effects=True, vmem_limit_bytes=56 * 1024 * 1024
        ),
        cost_estimate=pl.CostEstimate(flops=2 * 2048 * 4096 * 1024, bytes_accessed=7 * 2**20, transcendentals=0),
    )(amp_mask, pair_map, int_mask, amplitudes.reshape(32, TILE, 128), integrals)


def solution(mesh):
    in_specs = (P("row", "col"), P("row", "col"), P(), P(), P())
    out_specs = P("row", "col")
    return jax.shard_map(local, mesh=mesh, in_specs=in_specs, out_specs=out_specs, check_vma=False)
```

```python
import jax
import jax.numpy as jnp
from jax import lax
from jax.experimental import pallas as pl
from jax.experimental.pallas import tpu as pltpu
from jax.sharding import PartitionSpec as P

TILE = 64
HALF = TILE // 2
MESH = pl.DeviceIdType.MESH
CHUNKS = 4
WIDE = 256
ROWS_STEP = 512
RINGS = CHUNKS + 10
RELAYS = 31


class Ring:
    def __init__(self, slot, down, up, send, recv):
        routes = (
            (slot(0, 0), up),
            (slot(0, 1), down),
            (slot(0, 1), up),
            (slot(0, 0), down),
            (slot(-1, 0), up),
            (slot(1, 1), down),
        )
        self.copies = [
            pltpu.make_async_remote_copy(
                src_ref=piece, dst_ref=piece, send_sem=send.at[i], recv_sem=recv.at[i], device_id=to, device_id_type=MESH
            )
            for i, (piece, to) in enumerate(routes)
        ]

    def start_first(self):
        for copy in self.copies[:2]:
            copy.start()

    def start_second(self):
        for copy in self.copies[2:4]:
            copy.start()

    def start(self):
        self.start_first()
        self.start_second()

    def forward(self):
        for i in (0, 1):
            self.copies[i].wait_recv()
            self.copies[4 + i].start()

    def near(self):
        for copy in self.copies[2:4]:
            copy.wait_recv()

    def far(self):
        for copy in self.copies[4:]:
            copy.wait_recv()

    def finish(self):
        for copy in self.copies:
            copy.wait_send()


def kernel(
    amp_mask_in, pair_map_in, int_mask_in, amp, ints, out,
    amp_mask, pair_map, int_mask, known_0, known_1, packed_0, packed_1, got_0, got_1,
    full, ints_in, flag_rows, ints_all, total,
    ring_send, ring_recv, swap_send, swap_recv, relay_send, relay_recv, local_sem,
):
    y = lax.axis_index("row")
    col = lax.axis_index("col")
    core = lax.rem(col, 2)
    x = lax.rem(lax.div(col, 2), 4)
    z = lax.div(col, 8)

    def turn(a, d):
        return lax.rem(a + (d + 4), 4)

    def place(dx, dz, c):
        return turn(z, dz) * 8 + turn(x, dx) * 2 + c

    up_y, down_y = (turn(y, 1), col), (turn(y, -1), col)
    up_x, down_x = (y, place(1, 0, core)), (y, place(-1, 0, core))
    up_z, down_z = (y, place(0, 1, core)), (y, place(0, -1, core))
    twin = (y, place(0, 0, 1 - core))

    barrier = pltpu.get_barrier_semaphore()
    for other in (up_y, down_y, up_x, down_x, up_z, down_z, twin):
        pl.semaphore_signal(barrier, inc=1, device_id=other, device_id_type=MESH)

    known, packed, got = (known_0, known_1), (packed_0, packed_1), (got_0, got_1)

    def half_rows(h):
        return amp.at[:, pl.ds(h * HALF, HALF)]

    mask_row = pl.multiple_of(lax.div(col, 4) * 8, 8)
    own_row = pl.multiple_of(y * 16, 16)
    ints_copy = pltpu.make_async_copy(ints, ints_in, local_sem.at[0])
    int_mask_copy = pltpu.make_async_copy(int_mask_in.at[pl.ds(own_row, 16)], int_mask, local_sem.at[1])
    amp_copies = [
        pltpu.make_async_copy(amp_mask_in.at[pl.ds(mask_row, 8)], amp_mask, local_sem.at[2]),
        pltpu.make_async_copy(pair_map_in, pair_map, local_sem.at[3]),
        pltpu.make_async_copy(half_rows(0), known_0.at[pl.ds(0, 32)], local_sem.at[4]),
        pltpu.make_async_copy(half_rows(1), known_1.at[pl.ds(0, 32)], local_sem.at[5]),
    ]
    for copy in (int_mask_copy, ints_copy, *amp_copies):
        copy.start()

    odd = lax.rem(y, 2)
    even_odd = y + 1 - 2 * odd
    odd_even = lax.rem(y + 3 + 2 * odd, 4)
    first, second = (even_odd, odd_even), (odd_even, even_odd)

    def swap(n, src, dst, to):
        return pltpu.make_async_remote_copy(
            src_ref=src, dst_ref=dst, send_sem=swap_send.at[n], recv_sem=swap_recv.at[n],
            device_id=(to, col), device_id_type=MESH,
        )

    swap_all = [swap(h, half_rows(h), known[h].at[pl.ds(32, 32)], first[h]) for h in (0, 1)]
    swap_some = [swap(2 + h, packed[h], got[h], second[h]) for h in (0, 1)]

    pl.semaphore_wait(barrier, 7)
    for copy in swap_all:
        copy.start()

    wide = CHUNKS * WIDE
    chosen = lax.broadcasted_iota(jnp.int32, (512, wide), 0)
    lane_tile = lax.broadcasted_iota(jnp.int32, (512, wide), 1) >> 6
    pick = jnp.where(chosen == lane_tile + col * 16, 1.0, 0.0).astype(jnp.bfloat16)
    int_mask_copy.wait()
    flags = int_mask[...].astype(jnp.float32).astype(jnp.bfloat16)
    flag_rows[...] = jnp.dot(flags, pick, preferred_element_type=jnp.float32)
    ints_copy.wait()

    def mask_chunk(j):
        for t in range(16):
            flag = flag_rows[t : t + 1, j * WIDE : (j + 1) * WIDE]
            spread = jnp.broadcast_to(flag, (TILE, WIDE)).astype(jnp.bfloat16)
            block = ints_in[t * TILE : (t + 1) * TILE, j * WIDE : (j + 1) * WIDE]
            ints_all[j, pl.ds(pl.multiple_of(y * 1024 + t * TILE, TILE), TILE), :] = block * spread

    used = [0]

    def ring(slot, down, up):
        n = used[0]
        used[0] += 1
        return Ring(slot, down, up, ring_send.at[n], ring_recv.at[n])

    def ring_of_chunk(j):
        return ring(
            lambda d, half: ints_all.at[j, pl.ds(pl.multiple_of(turn(y, d) * 1024 + half * 512, 512), 512)],
            down_y, up_y,
        )

    ring_b = [ring_of_chunk(j) for j in range(CHUNKS)]

    mask_chunk(0)
    ring_b[0].start_first()

    for copy in amp_copies:
        copy.wait()
    for h in (0, 1):
        swap_all[h].wait_recv()

        def pack(q, carry, h=h):
            tile = pair_map[second[h] * 32 + q]
            plane, at = tile >> 5, tile & 31
            here = jnp.where(plane == y, at, jnp.where(plane == first[h], at + 32, 0))
            packed[h][q] = known[h][here]
            return carry

        lax.fori_loop(0, 32, pack, 0)
        swap_some[h].start()
    ring_b[0].start_second()
    for j in range(1, CHUNKS):
        mask_chunk(j)
    for copy in swap_some:
        copy.wait_recv()

    lane = lax.broadcasted_iota(jnp.int32, (HALF, 128), 1)

    def choose(q, carry):
        tile = pair_map[y * 32 + q]
        plane, at = tile >> 5, tile & 31
        left = amp_mask[lax.rem(col, 4) * 2, tile]
        right = amp_mask[lax.rem(col, 4) * 2 + 1, tile]
        for h in (0, 1):
            mine = jnp.where(plane == y, 1, 0)
            theirs = jnp.where(plane == first[h], 1, 0)
            here = mine + theirs
            there = 1 - here

            def flag(side):
                return jnp.where(lane < TILE, left * side, right * side).astype(jnp.float32).astype(jnp.bfloat16)

            full[col, pl.ds(pl.multiple_of(q * TILE + h * HALF, HALF), HALF), :] = (
                known[h][at + 32 * theirs] * flag(here) + got[h][q] * flag(there)
            )
        return carry

    lax.fori_loop(0, 32, choose, 0)

    relays = []

    def relay(dx, dz, start, size):
        n = len(relays)
        piece = full.at[place(dx, dz, core), pl.ds(start, size)]
        copy = pltpu.make_async_remote_copy(
            src_ref=piece, dst_ref=piece, send_sem=relay_send.at[n], recv_sem=relay_recv.at[n],
            device_id=twin, device_id_type=MESH,
        )
        copy.start()
        relays.append(copy)

    def rows_of(part, half):
        return pl.ds(part * 1024 + half * 512, 512)

    def ring_x(part, dz):
        return ring(lambda d, half: full.at[place(d, dz, core), rows_of(part, half)], down_x, up_x)

    def ring_z(part, dx):
        return ring(lambda d, half: full.at[place(dx, d, core), rows_of(part, half)], down_z, up_z)

    first_x, first_z = ring_x(0, 0), ring_z(1, 0)
    then_z = {d: ring_z(0, d) for d in (0, -1, 1, 2)}
    then_x = {d: ring_x(1, d) for d in (0, -1, 1, 2)}
    first_x.start()
    first_z.start()
    relay(0, 0, 0, 2048)
    then_z[0].start()
    then_x[0].start()
    first_x.forward()
    first_z.forward()
    ring_b[0].forward()
    ring_b[1].start()
    first_x.near()
    first_z.near()
    for d in (-1, 1):
        then_z[d].start()
        then_x[d].start()
        relay(d, 0, 0, 1024)
        relay(0, d, 1024, 1024)
    first_x.far()
    first_z.far()
    then_z[2].start()
    then_x[2].start()
    relay(2, 0, 0, 1024)
    relay(0, 2, 1024, 1024)
    for d in (0, -1, 1, 2):
        then_z[d].forward()
        then_x[d].forward()
        then_z[d].near()
        then_x[d].near()
        for e in (-1, 1):
            relay(d, e, 0, 1024)
            relay(e, d, 1024, 1024)
        if d == -1:
            ring_b[1].forward()
            ring_b[2].start()
    for d in (0, -1, 1, 2):
        then_z[d].far()
        then_x[d].far()
        relay(d, 2, 0, 1024)
        relay(2, d, 1024, 1024)
    ring_b[2].forward()
    ring_b[3].start()
    for copy in relays:
        copy.wait_recv()

    def lines(m):
        return pl.ds(pl.multiple_of(m * ROWS_STEP, ROWS_STEP), ROWS_STEP)

    def over_rows(body):
        def step(m, carry):
            body(lines(m))
            return carry

        lax.fori_loop(0, 2048 // ROWS_STEP, step, 0)

    def whole(j):
        def body(rows):
            left = jnp.concatenate([full[s, rows, :] for s in range(32)], axis=1)
            out[rows, j * WIDE : (j + 1) * WIDE] = jnp.dot(
                left, ints_all[j], preferred_element_type=jnp.float32
            ).astype(jnp.bfloat16)

        over_rows(body)

    last = CHUNKS - 1

    def part(d, rows):
        plane = turn(y, d)
        left = jnp.concatenate([full[plane * 8 + s, rows, :] for s in range(8)], axis=1)
        right = ints_all[last, pl.ds(pl.multiple_of(plane * 1024, 1024), 1024), :]
        return jnp.dot(left, right, preferred_element_type=jnp.float32)

    def begin(rows):
        total[rows, :] = part(0, rows)

    def add(rows):
        total[rows, :] += part(-1, rows) + part(1, rows)

    def end(rows):
        out[rows, last * WIDE : (last + 1) * WIDE] = (total[rows, :] + part(2, rows)).astype(jnp.bfloat16)

    ring_b[0].near()
    ring_b[0].far()
    whole(0)
    ring_b[1].near()
    ring_b[1].far()
    whole(1)
    ring_b[3].forward()
    ring_b[2].near()
    ring_b[2].far()
    whole(2)
    over_rows(begin)
    ring_b[3].near()
    over_rows(add)
    ring_b[3].far()
    over_rows(end)

    for each in (*ring_b, first_x, first_z, *then_z.values(), *then_x.values()):
        each.finish()
    for copy in (*swap_all, *swap_some, *relays):
        copy.wait_send()


def local(amplitudes, integrals, amp_mask, int_mask, pair_map):
    anywhere = pl.BlockSpec(memory_space=pl.ANY)
    half_tiles = [pltpu.VMEM((n, HALF, 128), jnp.bfloat16) for n in (64, 64, 32, 32, 32, 32)]
    return pl.pallas_call(
        kernel,
        out_shape=pltpu.VMEM((2048, 1024), jnp.bfloat16),
        in_specs=[anywhere] * 5,
        out_specs=pl.BlockSpec(memory_space=pltpu.VMEM),
        scratch_shapes=[
            pltpu.SMEM((8, 128), jnp.int32),
            pltpu.SMEM((128,), jnp.int32),
            pltpu.VMEM((16, 512), jnp.int32),
            *half_tiles,
            pltpu.VMEM((32, 2048, 128), jnp.bfloat16),
            pltpu.VMEM((1024, 1024), jnp.bfloat16),
            pltpu.VMEM((16, 1024), jnp.float32),
            pltpu.VMEM((CHUNKS, 4096, WIDE), jnp.bfloat16),
            pltpu.VMEM((2048, WIDE), jnp.float32),
            pltpu.SemaphoreType.DMA((RINGS, 6)),
            pltpu.SemaphoreType.DMA((RINGS, 6)),
            pltpu.SemaphoreType.DMA((4,)),
            pltpu.SemaphoreType.DMA((4,)),
            pltpu.SemaphoreType.DMA((RELAYS,)),
            pltpu.SemaphoreType.DMA((RELAYS,)),
            pltpu.SemaphoreType.DMA((6,)),
        ],
        compiler_params=pltpu.CompilerParams(
            collective_id=0, has_side_effects=True, vmem_limit_bytes=52 * 1024 * 1024
        ),
        cost_estimate=pl.CostEstimate(flops=2 * 2048 * 4096 * 1024, bytes_accessed=7 * 2**20, transcendentals=0),
    )(amp_mask.T, pair_map, int_mask, amplitudes.reshape(32, TILE, 128), integrals)


def solution(mesh):
    in_specs = (P("row", "col"), P("row", "col"), P(), P(), P())
    out_specs = P("row", "col")
    return jax.shard_map(local, mesh=mesh, in_specs=in_specs, out_specs=out_specs, check_vma=False)
```

```python
import jax
import jax.numpy as jnp
from jax import lax
from jax.experimental import pallas as pl
from jax.experimental.pallas import tpu as pltpu
from jax.sharding import PartitionSpec as P

TILE = 64
HALF = TILE // 2
MESH = pl.DeviceIdType.MESH
CHUNKS = 4
EARLY = 2
WIDE = 256
ROWS_STEP = 512
RINGS = CHUNKS + 10
RELAYS = 31


class Ring:
    def __init__(self, slot, down, up, send, recv):
        routes = (
            (slot(0, 0), up),
            (slot(0, 1), down),
            (slot(0, 1), up),
            (slot(0, 0), down),
            (slot(-1, 0), up),
            (slot(1, 1), down),
        )
        self.copies = [
            pltpu.make_async_remote_copy(
                src_ref=piece, dst_ref=piece, send_sem=send.at[i], recv_sem=recv.at[i], device_id=to, device_id_type=MESH
            )
            for i, (piece, to) in enumerate(routes)
        ]

    def start_first(self):
        for copy in self.copies[:2]:
            copy.start()

    def start_second(self):
        for copy in self.copies[2:4]:
            copy.start()

    def start(self):
        self.start_first()
        self.start_second()

    def forward(self):
        for i in (0, 1):
            self.copies[i].wait_recv()
            self.copies[4 + i].start()

    def near(self):
        for copy in self.copies[2:4]:
            copy.wait_recv()

    def far(self):
        for copy in self.copies[4:]:
            copy.wait_recv()

    def finish(self):
        for copy in self.copies:
            copy.wait_send()


def kernel(
    amp_mask_in, pair_map_in, int_mask_in, amp, ints, out,
    amp_mask, pair_map, int_mask, known_0, known_1, packed_0, packed_1, got_0, got_1,
    full, ints_in, flag_rows, ints_all, early, total,
    ring_send, ring_recv, swap_send, swap_recv, relay_send, relay_recv, local_sem,
):
    y = lax.axis_index("row")
    col = lax.axis_index("col")
    core = lax.rem(col, 2)
    x = lax.rem(lax.div(col, 2), 4)
    z = lax.div(col, 8)

    def turn(a, d):
        return lax.rem(a + (d + 4), 4)

    def place(dx, dz, c):
        return turn(z, dz) * 8 + turn(x, dx) * 2 + c

    up_y, down_y = (turn(y, 1), col), (turn(y, -1), col)
    up_x, down_x = (y, place(1, 0, core)), (y, place(-1, 0, core))
    up_z, down_z = (y, place(0, 1, core)), (y, place(0, -1, core))
    twin = (y, place(0, 0, 1 - core))

    barrier = pltpu.get_barrier_semaphore()
    for other in (up_y, down_y, up_x, down_x, up_z, down_z, twin):
        pl.semaphore_signal(barrier, inc=1, device_id=other, device_id_type=MESH)

    known, packed, got = (known_0, known_1), (packed_0, packed_1), (got_0, got_1)

    def half_rows(h):
        return amp.at[:, pl.ds(h * HALF, HALF)]

    mask_row = pl.multiple_of(lax.div(col, 4) * 8, 8)
    own_row = pl.multiple_of(y * 16, 16)
    ints_copy = pltpu.make_async_copy(ints, ints_in, local_sem.at[0])
    int_mask_copy = pltpu.make_async_copy(int_mask_in.at[pl.ds(own_row, 16)], int_mask, local_sem.at[1])
    amp_copies = [
        pltpu.make_async_copy(amp_mask_in.at[pl.ds(mask_row, 8)], amp_mask, local_sem.at[2]),
        pltpu.make_async_copy(pair_map_in, pair_map, local_sem.at[3]),
        pltpu.make_async_copy(half_rows(0), known_0.at[pl.ds(0, 32)], local_sem.at[4]),
        pltpu.make_async_copy(half_rows(1), known_1.at[pl.ds(0, 32)], local_sem.at[5]),
    ]
    for copy in (int_mask_copy, ints_copy, *amp_copies):
        copy.start()

    odd = lax.rem(y, 2)
    even_odd = y + 1 - 2 * odd
    odd_even = lax.rem(y + 3 + 2 * odd, 4)
    first, second = (even_odd, odd_even), (odd_even, even_odd)

    def swap(n, src, dst, to):
        return pltpu.make_async_remote_copy(
            src_ref=src, dst_ref=dst, send_sem=swap_send.at[n], recv_sem=swap_recv.at[n],
            device_id=(to, col), device_id_type=MESH,
        )

    swap_all = [swap(h, half_rows(h), known[h].at[pl.ds(32, 32)], first[h]) for h in (0, 1)]
    swap_some = [swap(2 + h, packed[h], got[h], second[h]) for h in (0, 1)]

    pl.semaphore_wait(barrier, 7)
    for copy in swap_all:
        copy.start()

    wide = CHUNKS * WIDE
    chosen = lax.broadcasted_iota(jnp.int32, (512, wide), 0)
    lane_tile = lax.broadcasted_iota(jnp.int32, (512, wide), 1) >> 6
    pick = jnp.where(chosen == lane_tile + col * 16, 1.0, 0.0).astype(jnp.bfloat16)
    int_mask_copy.wait()
    flags = int_mask[...].astype(jnp.float32).astype(jnp.bfloat16)
    flag_rows[...] = jnp.dot(flags, pick, preferred_element_type=jnp.float32)
    ints_copy.wait()

    def mask_chunk(j):
        for t in range(16):
            flag = flag_rows[t : t + 1, j * WIDE : (j + 1) * WIDE]
            spread = jnp.broadcast_to(flag, (TILE, WIDE)).astype(jnp.bfloat16)
            block = ints_in[t * TILE : (t + 1) * TILE, j * WIDE : (j + 1) * WIDE]
            ints_all[j, pl.ds(pl.multiple_of(y * 1024 + t * TILE, TILE), TILE), :] = block * spread

    used = [0]

    def ring(slot, down, up):
        n = used[0]
        used[0] += 1
        return Ring(slot, down, up, ring_send.at[n], ring_recv.at[n])

    def ring_of_chunk(j):
        return ring(
            lambda d, half: ints_all.at[j, pl.ds(pl.multiple_of(turn(y, d) * 1024 + half * 512, 512), 512)],
            down_y, up_y,
        )

    ring_b = [ring_of_chunk(j) for j in range(CHUNKS)]

    mask_chunk(0)
    ring_b[0].start_first()

    for copy in amp_copies:
        copy.wait()
    for h in (0, 1):
        swap_all[h].wait_recv()

        def pack(q, carry, h=h):
            tile = pair_map[second[h] * 32 + q]
            plane, at = tile >> 5, tile & 31
            here = jnp.where(plane == y, at, jnp.where(plane == first[h], at + 32, 0))
            packed[h][q] = known[h][here]
            return carry

        lax.fori_loop(0, 32, pack, 0)
        swap_some[h].start()
    ring_b[0].start_second()
    for j in range(1, CHUNKS):
        mask_chunk(j)
    ring_b[0].forward()
    ring_b[1].start()
    for copy in swap_some:
        copy.wait_recv()

    lane = lax.broadcasted_iota(jnp.int32, (HALF, 128), 1)

    def choose(q, carry):
        tile = pair_map[y * 32 + q]
        plane, at = tile >> 5, tile & 31
        left = amp_mask[lax.rem(col, 4) * 2, tile]
        right = amp_mask[lax.rem(col, 4) * 2 + 1, tile]
        for h in (0, 1):
            mine = jnp.where(plane == y, 1, 0)
            theirs = jnp.where(plane == first[h], 1, 0)
            here = mine + theirs
            there = 1 - here

            def flag(side):
                return jnp.where(lane < TILE, left * side, right * side).astype(jnp.float32).astype(jnp.bfloat16)

            full[col, pl.ds(pl.multiple_of(q * TILE + h * HALF, HALF), HALF), :] = (
                known[h][at + 32 * theirs] * flag(here) + got[h][q] * flag(there)
            )
        return carry

    lax.fori_loop(0, 32, choose, 0)

    relays = {}

    def relay(dx, dz, start, size):
        n = len(relays)
        part = start // 1024
        piece = full.at[place(dx, dz, core), pl.ds(start, size)]
        copy = pltpu.make_async_remote_copy(
            src_ref=piece, dst_ref=piece, send_sem=relay_send.at[n], recv_sem=relay_recv.at[n],
            device_id=twin, device_id_type=MESH,
        )
        copy.start()
        relays[dx, dz, part] = copy

    def rows_of(part, half):
        return pl.ds(part * 1024 + half * 512, 512)

    def ring_x(part, dz):
        return ring(lambda d, half: full.at[place(d, dz, core), rows_of(part, half)], down_x, up_x)

    def ring_z(part, dx):
        return ring(lambda d, half: full.at[place(dx, d, core), rows_of(part, half)], down_z, up_z)

    first_x, first_z = ring_x(0, 0), ring_z(1, 0)
    then_z = {d: ring_z(0, d) for d in (0, -1, 1, 2)}
    then_x = {d: ring_x(1, d) for d in (0, -1, 1, 2)}
    first_x.start()
    first_z.start()
    relay(0, 0, 0, 2048)
    then_z[0].start()
    then_x[0].start()
    first_x.forward()
    first_z.forward()
    first_x.near()
    first_z.near()
    for d in (-1, 1):
        then_z[d].start()
        then_x[d].start()
        relay(d, 0, 0, 1024)
        relay(0, d, 1024, 1024)
    first_x.far()
    first_z.far()
    then_z[2].start()
    then_x[2].start()
    relay(2, 0, 0, 1024)
    relay(0, 2, 1024, 1024)
    for d in (0, -1, 1, 2):
        then_z[d].forward()
        then_x[d].forward()
        then_z[d].near()
        then_x[d].near()
        for e in (-1, 1):
            relay(d, e, 0, 1024)
            relay(e, d, 1024, 1024)
        if d == -1:
            ring_b[1].forward()
            ring_b[2].start()
    def lines(m):
        return pl.ds(pl.multiple_of(m * ROWS_STEP, ROWS_STEP), ROWS_STEP)

    def over_rows(body, start=0, stop=2048):
        def step(m, carry):
            body(lines(m))
            return carry

        lax.fori_loop(start // ROWS_STEP, stop // ROWS_STEP, step, 0)

    def quarter(d):
        for share in range(2):
            if share == 0:
                runs = [(pl.multiple_of((zz * 8 + turn(x, d) * 2) * 128, 256), 2) for zz in range(4)]
            else:
                runs = [(pl.multiple_of(turn(z, d) * 1024, 1024), 8)]

            def body(rows):
                left = jnp.concatenate(
                    [full[at // 128 + s, rows, :] for at, n in runs for s in range(n)], axis=1
                )
                for j in range(EARLY):
                    right = jnp.concatenate([ints_all[j, pl.ds(at, n * 128), :] for at, n in runs], axis=0)
                    here = jnp.dot(left, right, preferred_element_type=jnp.float32)
                    if d != 0:
                        here = here + early[j, rows, :]
                    if d != 2:
                        early[j, rows, :] = here
                    else:
                        out[rows, j * WIDE : (j + 1) * WIDE] = here.astype(jnp.bfloat16)

            over_rows(body, share * 1024, (share + 1) * 1024)

    def relayed(d):
        for e in (0, -1, 1, 2):
            relays[d, e, 0].wait_recv()
            if (e, d) != (0, 0):
                relays[e, d, 1].wait_recv()

    for j in range(EARLY):
        ring_b[j].near()
        ring_b[j].far()
    before = None
    for d in (0, -1, 1, 2):
        then_z[d].far()
        then_x[d].far()
        relay(d, 2, 0, 1024)
        relay(2, d, 1024, 1024)
        if d == 0:
            ring_b[2].forward()
            ring_b[3].start()
        else:
            relayed(before)
            quarter(before)
        before = d
    relayed(before)
    quarter(before)

    def whole(j):
        def body(rows):
            left = jnp.concatenate([full[s, rows, :] for s in range(32)], axis=1)
            out[rows, j * WIDE : (j + 1) * WIDE] = jnp.dot(
                left, ints_all[j], preferred_element_type=jnp.float32
            ).astype(jnp.bfloat16)

        over_rows(body)

    last = CHUNKS - 1

    def part(d, rows):
        plane = turn(y, d)
        left = jnp.concatenate([full[plane * 8 + s, rows, :] for s in range(8)], axis=1)
        right = ints_all[last, pl.ds(pl.multiple_of(plane * 1024, 1024), 1024), :]
        return jnp.dot(left, right, preferred_element_type=jnp.float32)

    def begin(rows):
        total[rows, :] = part(0, rows)

    def add(rows):
        total[rows, :] += part(-1, rows) + part(1, rows)

    def end(rows):
        out[rows, last * WIDE : (last + 1) * WIDE] = (total[rows, :] + part(2, rows)).astype(jnp.bfloat16)

    ring_b[2].near()
    ring_b[2].far()
    ring_b[3].forward()
    whole(2)
    over_rows(begin)
    ring_b[3].near()
    over_rows(add)
    ring_b[3].far()
    over_rows(end)

    for each in (*ring_b, first_x, first_z, *then_z.values(), *then_x.values()):
        each.finish()
    for copy in (*swap_all, *swap_some, *relays.values()):
        copy.wait_send()


def local(amplitudes, integrals, amp_mask, int_mask, pair_map):
    anywhere = pl.BlockSpec(memory_space=pl.ANY)
    half_tiles = [pltpu.VMEM((n, HALF, 128), jnp.bfloat16) for n in (64, 64, 32, 32, 32, 32)]
    return pl.pallas_call(
        kernel,
        out_shape=pltpu.VMEM((2048, 1024), jnp.bfloat16),
        in_specs=[anywhere] * 5,
        out_specs=pl.BlockSpec(memory_space=pltpu.VMEM),
        scratch_shapes=[
            pltpu.SMEM((8, 128), jnp.int32),
            pltpu.SMEM((128,), jnp.int32),
            pltpu.VMEM((16, 512), jnp.int32),
            *half_tiles,
            pltpu.VMEM((32, 2048, 128), jnp.bfloat16),
            pltpu.VMEM((1024, 1024), jnp.bfloat16),
            pltpu.VMEM((16, 1024), jnp.float32),
            pltpu.VMEM((CHUNKS, 4096, WIDE), jnp.bfloat16),
            pltpu.VMEM((EARLY, 2048, WIDE), jnp.float32),
            pltpu.VMEM((2048, WIDE), jnp.float32),
            pltpu.SemaphoreType.DMA((RINGS, 6)),
            pltpu.SemaphoreType.DMA((RINGS, 6)),
            pltpu.SemaphoreType.DMA((4,)),
            pltpu.SemaphoreType.DMA((4,)),
            pltpu.SemaphoreType.DMA((RELAYS,)),
            pltpu.SemaphoreType.DMA((RELAYS,)),
            pltpu.SemaphoreType.DMA((6,)),
        ],
        compiler_params=pltpu.CompilerParams(
            collective_id=0, has_side_effects=True, vmem_limit_bytes=52 * 1024 * 1024
        ),
        cost_estimate=pl.CostEstimate(flops=2 * 2048 * 4096 * 1024, bytes_accessed=7 * 2**20, transcendentals=0),
    )(amp_mask.T, pair_map, int_mask, amplitudes.reshape(32, TILE, 128), integrals)


def solution(mesh):
    in_specs = (P("row", "col"), P("row", "col"), P(), P(), P())
    out_specs = P("row", "col")
    return jax.shard_map(local, mesh=mesh, in_specs=in_specs, out_specs=out_specs, check_vma=False)
```

```python
import jax
import jax.numpy as jnp
from jax import lax
from jax.experimental import pallas as pl
from jax.experimental.pallas import tpu as pltpu
from jax.sharding import PartitionSpec as P

TILE = 64
HALF = TILE // 2
MESH = pl.DeviceIdType.MESH
CHUNKS = 4
EARLY = 2
WIDE = 256
ROWS_STEP = 512
RINGS = CHUNKS + 10
RELAYS = 31


class Ring:
    def __init__(self, slot, down, up, send, recv):
        routes = (
            (slot(0, 0), up),
            (slot(0, 1), down),
            (slot(0, 1), up),
            (slot(0, 0), down),
            (slot(-1, 0), up),
            (slot(1, 1), down),
        )
        self.copies = [
            pltpu.make_async_remote_copy(
                src_ref=piece, dst_ref=piece, send_sem=send.at[i], recv_sem=recv.at[i], device_id=to, device_id_type=MESH
            )
            for i, (piece, to) in enumerate(routes)
        ]

    def start_first(self):
        for copy in self.copies[:2]:
            copy.start()

    def start_second(self):
        for copy in self.copies[2:4]:
            copy.start()

    def start(self):
        self.start_first()
        self.start_second()

    def forward(self):
        for i in (0, 1):
            self.copies[i].wait_recv()
            self.copies[4 + i].start()

    def near(self):
        for copy in self.copies[2:4]:
            copy.wait_recv()

    def far(self):
        for copy in self.copies[4:]:
            copy.wait_recv()

    def finish(self):
        for copy in self.copies:
            copy.wait_send()


def kernel(
    amp_mask_in, pair_map_in, int_mask_in, amp, ints, out,
    amp_mask, pair_map, int_mask, known_0, known_1, packed_0, packed_1, got_0, got_1,
    full, ints_in, flag_rows, ints_all, early, total,
    ring_send, ring_recv, swap_send, swap_recv, relay_send, relay_recv, local_sem,
):
    y = lax.axis_index("row")
    col = lax.axis_index("col")
    core = lax.rem(col, 2)
    x = lax.rem(lax.div(col, 2), 4)
    z = lax.div(col, 8)

    def turn(a, d):
        return lax.rem(a + (d + 4), 4)

    def place(dx, dz, c):
        return turn(z, dz) * 8 + turn(x, dx) * 2 + c

    up_y, down_y = (turn(y, 1), col), (turn(y, -1), col)
    up_x, down_x = (y, place(1, 0, core)), (y, place(-1, 0, core))
    up_z, down_z = (y, place(0, 1, core)), (y, place(0, -1, core))
    twin = (y, place(0, 0, 1 - core))

    barrier = pltpu.get_barrier_semaphore()
    for other in (up_y, down_y, up_x, down_x, up_z, down_z, twin):
        pl.semaphore_signal(barrier, inc=1, device_id=other, device_id_type=MESH)

    known, packed, got = (known_0, known_1), (packed_0, packed_1), (got_0, got_1)

    def half_rows(h):
        return amp.at[:, pl.ds(h * HALF, HALF)]

    mask_row = pl.multiple_of(lax.div(col, 4) * 8, 8)
    own_row = pl.multiple_of(y * 16, 16)
    ints_copy = pltpu.make_async_copy(ints, ints_in, local_sem.at[0])
    int_mask_copy = pltpu.make_async_copy(int_mask_in.at[pl.ds(own_row, 16)], int_mask, local_sem.at[1])
    amp_copies = [
        pltpu.make_async_copy(amp_mask_in.at[pl.ds(mask_row, 8)], amp_mask, local_sem.at[2]),
        pltpu.make_async_copy(pair_map_in, pair_map, local_sem.at[3]),
        pltpu.make_async_copy(half_rows(0), known_0.at[pl.ds(0, 32)], local_sem.at[4]),
        pltpu.make_async_copy(half_rows(1), known_1.at[pl.ds(0, 32)], local_sem.at[5]),
    ]
    for copy in (int_mask_copy, ints_copy, *amp_copies):
        copy.start()

    odd = lax.rem(y, 2)
    even_odd = y + 1 - 2 * odd
    odd_even = lax.rem(y + 3 + 2 * odd, 4)
    first, second = (even_odd, odd_even), (odd_even, even_odd)

    def swap(n, src, dst, to):
        return pltpu.make_async_remote_copy(
            src_ref=src, dst_ref=dst, send_sem=swap_send.at[n], recv_sem=swap_recv.at[n],
            device_id=(to, col), device_id_type=MESH,
        )

    swap_all = [swap(h, half_rows(h), known[h].at[pl.ds(32, 32)], first[h]) for h in (0, 1)]
    swap_some = [swap(2 + h, packed[h], got[h], second[h]) for h in (0, 1)]

    pl.semaphore_wait(barrier, 7)
    for copy in swap_all:
        copy.start()

    wide = CHUNKS * WIDE
    chosen = lax.broadcasted_iota(jnp.int32, (512, wide), 0)
    lane_tile = lax.broadcasted_iota(jnp.int32, (512, wide), 1) >> 6
    pick = jnp.where(chosen == lane_tile + col * 16, 1.0, 0.0).astype(jnp.bfloat16)
    int_mask_copy.wait()
    flags = int_mask[...].astype(jnp.float32).astype(jnp.bfloat16)
    flag_rows[...] = jnp.dot(flags, pick, preferred_element_type=jnp.float32)
    ints_copy.wait()

    def mask_chunk(j):
        for t in range(16):
            flag = flag_rows[t : t + 1, j * WIDE : (j + 1) * WIDE]
            spread = jnp.broadcast_to(flag, (TILE, WIDE)).astype(jnp.bfloat16)
            block = ints_in[t * TILE : (t + 1) * TILE, j * WIDE : (j + 1) * WIDE]
            ints_all[j, pl.ds(pl.multiple_of(y * 1024 + t * TILE, TILE), TILE), :] = block * spread

    used = [0]

    def ring(slot, down, up):
        n = used[0]
        used[0] += 1
        return Ring(slot, down, up, ring_send.at[n], ring_recv.at[n])

    def ring_of_chunk(j):
        return ring(
            lambda d, half: ints_all.at[j, pl.ds(pl.multiple_of(turn(y, d) * 1024 + half * 512, 512), 512)],
            down_y, up_y,
        )

    ring_b = [ring_of_chunk(j) for j in range(CHUNKS)]

    mask_chunk(0)
    ring_b[0].start_first()

    for copy in amp_copies:
        copy.wait()
    for h in (0, 1):
        swap_all[h].wait_recv()

        def pack(q, carry, h=h):
            tile = pair_map[second[h] * 32 + q]
            plane, at = tile >> 5, tile & 31
            here = jnp.where(plane == y, at, jnp.where(plane == first[h], at + 32, 0))
            packed[h][q] = known[h][here]
            return carry

        lax.fori_loop(0, 32, pack, 0)
        swap_some[h].start()
    ring_b[0].start_second()
    for j in range(1, CHUNKS):
        mask_chunk(j)
    ring_b[0].forward()
    ring_b[1].start()
    for copy in swap_some:
        copy.wait_recv()

    lane = lax.broadcasted_iota(jnp.int32, (HALF, 128), 1)

    def choose(q, carry):
        tile = pair_map[y * 32 + q]
        plane, at = tile >> 5, tile & 31
        left = amp_mask[lax.rem(col, 4) * 2, tile]
        right = amp_mask[lax.rem(col, 4) * 2 + 1, tile]
        for h in (0, 1):
            mine = jnp.where(plane == y, 1, 0)
            theirs = jnp.where(plane == first[h], 1, 0)
            here = mine + theirs
            there = 1 - here

            def flag(side):
                return jnp.where(lane < TILE, left * side, right * side).astype(jnp.float32).astype(jnp.bfloat16)

            full[col, pl.ds(pl.multiple_of(q * TILE + h * HALF, HALF), HALF), :] = (
                known[h][at + 32 * theirs] * flag(here) + got[h][q] * flag(there)
            )
        return carry

    lax.fori_loop(0, 32, choose, 0)

    relays = {}

    def relay(dx, dz, start, size):
        n = len(relays)
        part = start // 1024
        piece = full.at[place(dx, dz, core), pl.ds(start, size)]
        copy = pltpu.make_async_remote_copy(
            src_ref=piece, dst_ref=piece, send_sem=relay_send.at[n], recv_sem=relay_recv.at[n],
            device_id=twin, device_id_type=MESH,
        )
        copy.start()
        relays[dx, dz, part] = copy

    def rows_of(part, half):
        return pl.ds(part * 1024 + half * 512, 512)

    def ring_x(part, dz):
        return ring(lambda d, half: full.at[place(d, dz, core), rows_of(part, half)], down_x, up_x)

    def ring_z(part, dx):
        return ring(lambda d, half: full.at[place(dx, d, core), rows_of(part, half)], down_z, up_z)

    first_x, first_z = ring_x(0, 0), ring_z(1, 0)
    then_z = {d: ring_z(0, d) for d in (0, -1, 1, 2)}
    then_x = {d: ring_x(1, d) for d in (0, -1, 1, 2)}
    first_x.start()
    first_z.start()
    relay(0, 0, 0, 2048)
    then_z[0].start()
    then_x[0].start()
    def lines(m):
        return pl.ds(pl.multiple_of(m * ROWS_STEP, ROWS_STEP), ROWS_STEP)

    def over_rows(body, start=0, stop=2048):
        def step(m, carry):
            body(lines(m))
            return carry

        lax.fori_loop(start // ROWS_STEP, stop // ROWS_STEP, step, 0)

    def quarter(d):
        for share in range(2):
            if share == 0:
                runs = [(pl.multiple_of((zz * 8 + turn(x, d) * 2) * 128, 256), 2) for zz in range(4)]
            else:
                runs = [(pl.multiple_of(turn(z, d) * 1024, 1024), 8)]

            def body(rows):
                left = jnp.concatenate(
                    [full[at // 128 + s, rows, :] for at, n in runs for s in range(n)], axis=1
                )
                for j in range(EARLY):
                    right = jnp.concatenate([ints_all[j, pl.ds(at, n * 128), :] for at, n in runs], axis=0)
                    here = jnp.dot(left, right, preferred_element_type=jnp.float32)
                    if d != 0:
                        here = here + early[j, rows, :]
                    if d != 2:
                        early[j, rows, :] = here
                    else:
                        out[rows, j * WIDE : (j + 1) * WIDE] = here.astype(jnp.bfloat16)

            over_rows(body, share * 1024, (share + 1) * 1024)

    def relayed(d):
        for e in (0, -1, 1, 2):
            relays[d, e, 0].wait_recv()
            if (e, d) != (0, 0):
                relays[e, d, 1].wait_recv()

    def whole(j, start, stop):
        def body(rows):
            left = jnp.concatenate([full[s, rows, :] for s in range(32)], axis=1)
            out[rows, j * WIDE : (j + 1) * WIDE] = jnp.dot(
                left, ints_all[j], preferred_element_type=jnp.float32
            ).astype(jnp.bfloat16)

        over_rows(body, start, stop)

    last = CHUNKS - 1

    def part(d, rows):
        plane = turn(y, d)
        left = jnp.concatenate([full[plane * 8 + s, rows, :] for s in range(8)], axis=1)
        right = ints_all[last, pl.ds(pl.multiple_of(plane * 1024, 1024), 1024), :]
        return jnp.dot(left, right, preferred_element_type=jnp.float32)

    def begin(rows):
        total[rows, :] = part(0, rows)

    def add(rows):
        total[rows, :] += part(-1, rows) + part(1, rows)

    def end(rows):
        out[rows, last * WIDE : (last + 1) * WIDE] = (total[rows, :] + part(2, rows)).astype(jnp.bfloat16)

    def near_two(d):
        then_z[d].near()
        then_x[d].near()
        for e in (-1, 1):
            relay(d, e, 0, 1024)
            relay(e, d, 1024, 1024)

    def far_two(d):
        then_z[d].far()
        then_x[d].far()
        relay(d, 2, 0, 1024)
        relay(2, d, 1024, 1024)

    def forward_two(d):
        then_z[d].forward()
        then_x[d].forward()

    def start_two(d):
        then_z[d].start()
        then_x[d].start()

    first_x.forward()
    first_z.forward()
    first_x.near()
    first_z.near()
    start_two(-1)
    for d in (-1, 1):
        relay(d, 0, 0, 1024)
        relay(0, d, 1024, 1024)
    forward_two(0)
    start_two(1)
    near_two(0)
    first_x.far()
    first_z.far()
    relay(2, 0, 0, 1024)
    relay(0, 2, 1024, 1024)
    ring_b[1].forward()
    ring_b[2].start()
    forward_two(-1)
    start_two(2)
    near_two(-1)
    far_two(0)
    for j in range(EARLY):
        ring_b[j].near()
        ring_b[j].far()
    forward_two(1)
    relayed(0)
    quarter(0)
    near_two(1)
    far_two(-1)
    ring_b[2].forward()
    ring_b[3].start()
    relayed(-1)
    quarter(-1)
    forward_two(2)
    near_two(2)
    far_two(1)
    relayed(1)
    quarter(1)
    far_two(2)
    ring_b[2].near()
    ring_b[2].far()
    relayed(2)
    quarter(2)
    whole(2, 0, 1024)
    ring_b[3].forward()
    whole(2, 1024, 2048)
    over_rows(begin)
    for each in (*ring_b[:3], first_x, first_z, *then_z.values(), *then_x.values()):
        each.finish()
    for copy in (*swap_all, *swap_some, *relays.values()):
        copy.wait_send()
    ring_b[3].near()
    over_rows(add)
    ring_b[3].far()
    over_rows(end)
    ring_b[3].finish()


def local(amplitudes, integrals, amp_mask, int_mask, pair_map):
    anywhere = pl.BlockSpec(memory_space=pl.ANY)
    half_tiles = [pltpu.VMEM((n, HALF, 128), jnp.bfloat16) for n in (64, 64, 32, 32, 32, 32)]
    return pl.pallas_call(
        kernel,
        out_shape=pltpu.VMEM((2048, 1024), jnp.bfloat16),
        in_specs=[anywhere] * 5,
        out_specs=pl.BlockSpec(memory_space=pltpu.VMEM),
        scratch_shapes=[
            pltpu.SMEM((8, 128), jnp.int32),
            pltpu.SMEM((128,), jnp.int32),
            pltpu.VMEM((16, 512), jnp.int32),
            *half_tiles,
            pltpu.VMEM((32, 2048, 128), jnp.bfloat16),
            pltpu.VMEM((1024, 1024), jnp.bfloat16),
            pltpu.VMEM((16, 1024), jnp.float32),
            pltpu.VMEM((CHUNKS, 4096, WIDE), jnp.bfloat16),
            pltpu.VMEM((EARLY, 2048, WIDE), jnp.float32),
            pltpu.VMEM((2048, WIDE), jnp.float32),
            pltpu.SemaphoreType.DMA((RINGS, 6)),
            pltpu.SemaphoreType.DMA((RINGS, 6)),
            pltpu.SemaphoreType.DMA((4,)),
            pltpu.SemaphoreType.DMA((4,)),
            pltpu.SemaphoreType.DMA((RELAYS,)),
            pltpu.SemaphoreType.DMA((RELAYS,)),
            pltpu.SemaphoreType.DMA((6,)),
        ],
        compiler_params=pltpu.CompilerParams(
            collective_id=0, has_side_effects=True, vmem_limit_bytes=52 * 1024 * 1024
        ),
        cost_estimate=pl.CostEstimate(flops=2 * 2048 * 4096 * 1024, bytes_accessed=7 * 2**20, transcendentals=0),
    )(amp_mask.T, pair_map, int_mask, amplitudes.reshape(32, TILE, 128), integrals)


def solution(mesh):
    in_specs = (P("row", "col"), P("row", "col"), P(), P(), P())
    out_specs = P("row", "col")
    return jax.shard_map(local, mesh=mesh, in_specs=in_specs, out_specs=out_specs, check_vma=False)
```

```python
import jax
import jax.numpy as jnp
from jax import lax
from jax.experimental import pallas as pl
from jax.experimental.pallas import tpu as pltpu
from jax.sharding import PartitionSpec as P

TILE = 64
HALF = TILE // 2
MESH = pl.DeviceIdType.MESH
CHUNKS = 4
EARLY = 2
WIDE = 256
WHOLE_STEP = 512
PART_STEP = 1024
LAST_STEP = 2048
RINGS = CHUNKS + 10
RELAYS = 31


class Ring:
    def __init__(self, slot, down, up, send, recv):
        routes = (
            (slot(0, 0), up),
            (slot(0, 1), down),
            (slot(0, 1), up),
            (slot(0, 0), down),
            (slot(-1, 0), up),
            (slot(1, 1), down),
        )
        self.copies = [
            pltpu.make_async_remote_copy(
                src_ref=piece, dst_ref=piece, send_sem=send.at[i], recv_sem=recv.at[i], device_id=to, device_id_type=MESH
            )
            for i, (piece, to) in enumerate(routes)
        ]

    def start_first(self):
        for copy in self.copies[:2]:
            copy.start()

    def start_second(self):
        for copy in self.copies[2:4]:
            copy.start()

    def start(self):
        self.start_first()
        self.start_second()

    def forward(self):
        for i in (0, 1):
            self.copies[i].wait_recv()
            self.copies[4 + i].start()

    def near(self):
        for copy in self.copies[2:4]:
            copy.wait_recv()

    def far(self):
        for copy in self.copies[4:]:
            copy.wait_recv()

    def finish(self):
        for copy in self.copies:
            copy.wait_send()


def kernel(
    amp_mask_in, pair_map_in, int_mask_in, amp, ints, out,
    amp_mask, pair_map, int_mask, known_0, known_1, packed_0, packed_1, got_0, got_1,
    full, ints_in, flag_rows, ints_all, early, total,
    ring_send, ring_recv, swap_send, swap_recv, relay_send, relay_recv, local_sem,
):
    y = lax.axis_index("row")
    col = lax.axis_index("col")
    core = lax.rem(col, 2)
    x = lax.rem(lax.div(col, 2), 4)
    z = lax.div(col, 8)

    def turn(a, d):
        return lax.rem(a + (d + 4), 4)

    def place(dx, dz, c):
        return turn(z, dz) * 8 + turn(x, dx) * 2 + c

    up_y, down_y = (turn(y, 1), col), (turn(y, -1), col)
    up_x, down_x = (y, place(1, 0, core)), (y, place(-1, 0, core))
    up_z, down_z = (y, place(0, 1, core)), (y, place(0, -1, core))
    twin = (y, place(0, 0, 1 - core))

    barrier = pltpu.get_barrier_semaphore()
    for other in (up_y, down_y, up_x, down_x, up_z, down_z, twin):
        pl.semaphore_signal(barrier, inc=1, device_id=other, device_id_type=MESH)

    known, packed, got = (known_0, known_1), (packed_0, packed_1), (got_0, got_1)

    def half_rows(h):
        return amp.at[:, pl.ds(h * HALF, HALF)]

    mask_row = pl.multiple_of(lax.div(col, 4) * 8, 8)
    own_row = pl.multiple_of(y * 16, 16)
    ints_copy = pltpu.make_async_copy(ints, ints_in, local_sem.at[0])
    int_mask_copy = pltpu.make_async_copy(int_mask_in.at[pl.ds(own_row, 16)], int_mask, local_sem.at[1])
    amp_copies = [
        pltpu.make_async_copy(amp_mask_in.at[pl.ds(mask_row, 8)], amp_mask, local_sem.at[2]),
        pltpu.make_async_copy(pair_map_in, pair_map, local_sem.at[3]),
        pltpu.make_async_copy(half_rows(0), known_0.at[pl.ds(0, 32)], local_sem.at[4]),
        pltpu.make_async_copy(half_rows(1), known_1.at[pl.ds(0, 32)], local_sem.at[5]),
    ]
    for copy in (int_mask_copy, ints_copy, *amp_copies):
        copy.start()

    odd = lax.rem(y, 2)
    even_odd = y + 1 - 2 * odd
    odd_even = lax.rem(y + 3 + 2 * odd, 4)
    first, second = (even_odd, odd_even), (odd_even, even_odd)

    def swap(n, src, dst, to):
        return pltpu.make_async_remote_copy(
            src_ref=src, dst_ref=dst, send_sem=swap_send.at[n], recv_sem=swap_recv.at[n],
            device_id=(to, col), device_id_type=MESH,
        )

    swap_all = [swap(h, half_rows(h), known[h].at[pl.ds(32, 32)], first[h]) for h in (0, 1)]
    swap_some = [swap(2 + h, packed[h], got[h], second[h]) for h in (0, 1)]

    pl.semaphore_wait(barrier, 7)
    for copy in swap_all:
        copy.start()

    wide = CHUNKS * WIDE
    chosen = lax.broadcasted_iota(jnp.int32, (512, wide), 0)
    lane_tile = lax.broadcasted_iota(jnp.int32, (512, wide), 1) >> 6
    pick = jnp.where(chosen == lane_tile + col * 16, 1.0, 0.0).astype(jnp.bfloat16)
    int_mask_copy.wait()
    flags = int_mask[...].astype(jnp.float32).astype(jnp.bfloat16)
    flag_rows[...] = jnp.dot(flags, pick, preferred_element_type=jnp.float32)
    ints_copy.wait()

    def mask_chunk(j):
        for t in range(16):
            flag = flag_rows[t : t + 1, j * WIDE : (j + 1) * WIDE]
            spread = jnp.broadcast_to(flag, (TILE, WIDE)).astype(jnp.bfloat16)
            block = ints_in[t * TILE : (t + 1) * TILE, j * WIDE : (j + 1) * WIDE]
            ints_all[j, pl.ds(pl.multiple_of(y * 1024 + t * TILE, TILE), TILE), :] = block * spread

    used = [0]

    def ring(slot, down, up):
        n = used[0]
        used[0] += 1
        return Ring(slot, down, up, ring_send.at[n], ring_recv.at[n])

    def ring_of_chunk(j):
        return ring(
            lambda d, half: ints_all.at[j, pl.ds(pl.multiple_of(turn(y, d) * 1024 + half * 512, 512), 512)],
            down_y, up_y,
        )

    ring_b = [ring_of_chunk(j) for j in range(CHUNKS)]

    mask_chunk(0)
    ring_b[0].start_first()

    for copy in amp_copies:
        copy.wait()
    for h in (0, 1):
        swap_all[h].wait_recv()

        def pack(q, carry, h=h):
            tile = pair_map[second[h] * 32 + q]
            plane, at = tile >> 5, tile & 31
            here = jnp.where(plane == y, at, jnp.where(plane == first[h], at + 32, 0))
            packed[h][q] = known[h][here]
            return carry

        lax.fori_loop(0, 32, pack, 0)
        swap_some[h].start()
    ring_b[0].start_second()
    for j in range(1, CHUNKS):
        mask_chunk(j)
    ring_b[0].forward()
    ring_b[1].start()
    for copy in swap_some:
        copy.wait_recv()

    lane = lax.broadcasted_iota(jnp.int32, (HALF, 128), 1)

    def choose(q, carry):
        tile = pair_map[y * 32 + q]
        plane, at = tile >> 5, tile & 31
        left = amp_mask[lax.rem(col, 4) * 2, tile]
        right = amp_mask[lax.rem(col, 4) * 2 + 1, tile]
        for h in (0, 1):
            mine = jnp.where(plane == y, 1, 0)
            theirs = jnp.where(plane == first[h], 1, 0)
            here = mine + theirs
            there = 1 - here

            def flag(side):
                return jnp.where(lane < TILE, left * side, right * side).astype(jnp.float32).astype(jnp.bfloat16)

            full[col, pl.ds(pl.multiple_of(q * TILE + h * HALF, HALF), HALF), :] = (
                known[h][at + 32 * theirs] * flag(here) + got[h][q] * flag(there)
            )
        return carry

    lax.fori_loop(0, 32, choose, 0)

    relays = {}

    def relay(dx, dz, start, size):
        n = len(relays)
        part = start // 1024
        piece = full.at[place(dx, dz, core), pl.ds(start, size)]
        copy = pltpu.make_async_remote_copy(
            src_ref=piece, dst_ref=piece, send_sem=relay_send.at[n], recv_sem=relay_recv.at[n],
            device_id=twin, device_id_type=MESH,
        )
        copy.start()
        relays[dx, dz, part] = copy

    def rows_of(part, half):
        return pl.ds(part * 1024 + half * 512, 512)

    def ring_x(part, dz):
        return ring(lambda d, half: full.at[place(d, dz, core), rows_of(part, half)], down_x, up_x)

    def ring_z(part, dx):
        return ring(lambda d, half: full.at[place(dx, d, core), rows_of(part, half)], down_z, up_z)

    first_x, first_z = ring_x(0, 0), ring_z(1, 0)
    then_z = {d: ring_z(0, d) for d in (0, -1, 1, 2)}
    then_x = {d: ring_x(1, d) for d in (0, -1, 1, 2)}
    first_x.start()
    first_z.start()
    relay(0, 0, 0, 2048)
    then_z[0].start()
    then_x[0].start()
    def over_rows(body, size, start=0, stop=2048):
        def step(m, carry):
            body(pl.ds(pl.multiple_of(m * size, size), size))
            return carry

        lax.fori_loop(start // size, stop // size, step, 0)

    def quarter(d):
        for share in range(2):
            if share == 0:
                runs = [(pl.multiple_of((zz * 8 + turn(x, d) * 2) * 128, 256), 2) for zz in range(4)]
            else:
                runs = [(pl.multiple_of(turn(z, d) * 1024, 1024), 8)]

            def body(rows):
                left = jnp.concatenate(
                    [full[at // 128 + s, rows, :] for at, n in runs for s in range(n)], axis=1
                )
                for j in range(EARLY):
                    right = jnp.concatenate([ints_all[j, pl.ds(at, n * 128), :] for at, n in runs], axis=0)
                    here = jnp.dot(left, right, preferred_element_type=jnp.float32)
                    if d != 0:
                        here = here + early[j, rows, :]
                    if d != 2:
                        early[j, rows, :] = here
                    else:
                        out[rows, j * WIDE : (j + 1) * WIDE] = here.astype(jnp.bfloat16)

            over_rows(body, PART_STEP, share * 1024, (share + 1) * 1024)

    def relayed(d):
        for e in (0, -1, 1, 2):
            relays[d, e, 0].wait_recv()
            if (e, d) != (0, 0):
                relays[e, d, 1].wait_recv()

    def whole(j, start, stop):
        def body(rows):
            left = jnp.concatenate([full[s, rows, :] for s in range(32)], axis=1)
            out[rows, j * WIDE : (j + 1) * WIDE] = jnp.dot(
                left, ints_all[j], preferred_element_type=jnp.float32
            ).astype(jnp.bfloat16)

        over_rows(body, WHOLE_STEP, start, stop)

    last = CHUNKS - 1

    def part(rows, *planes):
        starts = [turn(y, d) * 8 for d in planes]
        left = jnp.concatenate([full[start + s, rows, :] for start in starts for s in range(8)], axis=1)
        right = jnp.concatenate(
            [ints_all[last, pl.ds(pl.multiple_of(start * 128, 1024), 1024), :] for start in starts], axis=0
        )
        return jnp.dot(left, right, preferred_element_type=jnp.float32)

    def begin(rows):
        total[rows, :] = part(rows, 0)

    def add(rows):
        total[rows, :] += part(rows, -1, 1)

    def end(rows):
        out[rows, last * WIDE : (last + 1) * WIDE] = (total[rows, :] + part(rows, 2)).astype(jnp.bfloat16)

    def near_two(d):
        then_z[d].near()
        then_x[d].near()
        for e in (-1, 1):
            relay(d, e, 0, 1024)
            relay(e, d, 1024, 1024)

    def far_two(d):
        then_z[d].far()
        then_x[d].far()
        relay(d, 2, 0, 1024)
        relay(2, d, 1024, 1024)

    def forward_two(d):
        then_z[d].forward()
        then_x[d].forward()

    def start_two(d):
        then_z[d].start()
        then_x[d].start()

    first_x.forward()
    first_z.forward()
    first_x.near()
    first_z.near()
    start_two(-1)
    for d in (-1, 1):
        relay(d, 0, 0, 1024)
        relay(0, d, 1024, 1024)
    forward_two(0)
    start_two(1)
    near_two(0)
    first_x.far()
    first_z.far()
    relay(2, 0, 0, 1024)
    relay(0, 2, 1024, 1024)
    ring_b[1].forward()
    ring_b[2].start()
    forward_two(-1)
    start_two(2)
    near_two(-1)
    far_two(0)
    for j in range(EARLY):
        ring_b[j].near()
        ring_b[j].far()
    forward_two(1)
    relayed(0)
    quarter(0)
    near_two(1)
    far_two(-1)
    ring_b[2].forward()
    ring_b[3].start()
    relayed(-1)
    quarter(-1)
    forward_two(2)
    near_two(2)
    far_two(1)
    relayed(1)
    quarter(1)
    far_two(2)
    ring_b[2].near()
    ring_b[2].far()
    relayed(2)
    quarter(2)
    whole(2, 0, 1024)
    ring_b[3].forward()
    whole(2, 1024, 2048)
    over_rows(begin, PART_STEP)
    for each in (*ring_b[:3], first_x, first_z, *then_z.values(), *then_x.values()):
        each.finish()
    for copy in (*swap_all, *swap_some, *relays.values()):
        copy.wait_send()
    ring_b[3].near()
    over_rows(add, PART_STEP)
    ring_b[3].far()
    over_rows(end, LAST_STEP)
    ring_b[3].finish()


def local(amplitudes, integrals, amp_mask, int_mask, pair_map):
    anywhere = pl.BlockSpec(memory_space=pl.ANY)
    half_tiles = [pltpu.VMEM((n, HALF, 128), jnp.bfloat16) for n in (64, 64, 32, 32, 32, 32)]
    return pl.pallas_call(
        kernel,
        out_shape=pltpu.VMEM((2048, 1024), jnp.bfloat16),
        in_specs=[anywhere] * 5,
        out_specs=pl.BlockSpec(memory_space=pltpu.VMEM),
        scratch_shapes=[
            pltpu.SMEM((8, 128), jnp.int32),
            pltpu.SMEM((128,), jnp.int32),
            pltpu.VMEM((16, 512), jnp.int32),
            *half_tiles,
            pltpu.VMEM((32, 2048, 128), jnp.bfloat16),
            pltpu.VMEM((1024, 1024), jnp.bfloat16),
            pltpu.VMEM((16, 1024), jnp.float32),
            pltpu.VMEM((CHUNKS, 4096, WIDE), jnp.bfloat16),
            pltpu.VMEM((EARLY, 2048, WIDE), jnp.float32),
            pltpu.VMEM((2048, WIDE), jnp.float32),
            pltpu.SemaphoreType.DMA((RINGS, 6)),
            pltpu.SemaphoreType.DMA((RINGS, 6)),
            pltpu.SemaphoreType.DMA((4,)),
            pltpu.SemaphoreType.DMA((4,)),
            pltpu.SemaphoreType.DMA((RELAYS,)),
            pltpu.SemaphoreType.DMA((RELAYS,)),
            pltpu.SemaphoreType.DMA((6,)),
        ],
        compiler_params=pltpu.CompilerParams(
            collective_id=0, has_side_effects=True, vmem_limit_bytes=52 * 1024 * 1024
        ),
        cost_estimate=pl.CostEstimate(flops=2 * 2048 * 4096 * 1024, bytes_accessed=7 * 2**20, transcendentals=0),
    )(amp_mask.T, pair_map, int_mask, amplitudes.reshape(32, TILE, 128), integrals)


def solution(mesh):
    in_specs = (P("row", "col"), P("row", "col"), P(), P(), P())
    out_specs = P("row", "col")
    return jax.shard_map(local, mesh=mesh, in_specs=in_specs, out_specs=out_specs, check_vma=False)
```

```python
import jax
import jax.numpy as jnp
from jax import lax
from jax.experimental import pallas as pl
from jax.experimental.pallas import tpu as pltpu
from jax.sharding import PartitionSpec as P

TILE = 64
HALF = TILE // 2
MESH = pl.DeviceIdType.MESH
CHUNKS = 4
EARLY = 2
WIDE = 256
WHOLE_STEP = 512
PART_STEP = 1024
LAST_STEP = 2048
WRITES = 8
RINGS = CHUNKS + 10
RELAYS = 31


class Ring:
    def __init__(self, slot, down, up, send, recv):
        routes = (
            (slot(0, 0), up),
            (slot(0, 1), down),
            (slot(0, 1), up),
            (slot(0, 0), down),
            (slot(-1, 0), up),
            (slot(1, 1), down),
        )
        self.copies = [
            pltpu.make_async_remote_copy(
                src_ref=piece, dst_ref=piece, send_sem=send.at[i], recv_sem=recv.at[i], device_id=to, device_id_type=MESH
            )
            for i, (piece, to) in enumerate(routes)
        ]

    def start_first(self):
        for copy in self.copies[:2]:
            copy.start()

    def start_second(self):
        for copy in self.copies[2:4]:
            copy.start()

    def start(self):
        self.start_first()
        self.start_second()

    def forward(self):
        for i in (0, 1):
            self.copies[i].wait_recv()
            self.copies[4 + i].start()

    def near(self):
        for copy in self.copies[2:4]:
            copy.wait_recv()

    def far(self):
        for copy in self.copies[4:]:
            copy.wait_recv()

    def finish(self):
        for copy in self.copies:
            copy.wait_send()


def kernel(
    amp_mask_in, pair_map_in, int_mask_in, amp, ints, out,
    amp_mask, pair_map, int_mask, known_0, known_1, packed_0, packed_1, got_0, got_1,
    full, ints_in, flag_rows, ints_all, early, total,
    ring_send, ring_recv, swap_send, swap_recv, relay_send, relay_recv, local_sem,
):
    y = lax.axis_index("row")
    col = lax.axis_index("col")
    core = lax.rem(col, 2)
    x = lax.rem(lax.div(col, 2), 4)
    z = lax.div(col, 8)

    def turn(a, d):
        return lax.rem(a + (d + 4), 4)

    def place(dx, dz, c):
        return turn(z, dz) * 8 + turn(x, dx) * 2 + c

    up_y, down_y = (turn(y, 1), col), (turn(y, -1), col)
    up_x, down_x = (y, place(1, 0, core)), (y, place(-1, 0, core))
    up_z, down_z = (y, place(0, 1, core)), (y, place(0, -1, core))
    twin = (y, place(0, 0, 1 - core))

    barrier = pltpu.get_barrier_semaphore()
    for other in (up_y, down_y, up_x, down_x, up_z, down_z, twin):
        pl.semaphore_signal(barrier, inc=1, device_id=other, device_id_type=MESH)

    known, packed, got = (known_0, known_1), (packed_0, packed_1), (got_0, got_1)

    def half_rows(h):
        return amp.at[:, pl.ds(h * HALF, HALF)]

    mask_row = pl.multiple_of(lax.div(col, 4) * 8, 8)
    own_row = pl.multiple_of(y * 16, 16)
    ints_copy = pltpu.make_async_copy(ints, ints_in, local_sem.at[0])
    int_mask_copy = pltpu.make_async_copy(int_mask_in.at[pl.ds(own_row, 16)], int_mask, local_sem.at[1])
    amp_copies = [
        pltpu.make_async_copy(amp_mask_in.at[pl.ds(mask_row, 8)], amp_mask, local_sem.at[2]),
        pltpu.make_async_copy(pair_map_in, pair_map, local_sem.at[3]),
        pltpu.make_async_copy(half_rows(0), known_0.at[pl.ds(0, 32)], local_sem.at[4]),
        pltpu.make_async_copy(half_rows(1), known_1.at[pl.ds(0, 32)], local_sem.at[5]),
    ]
    for copy in (int_mask_copy, ints_copy, *amp_copies):
        copy.start()

    odd = lax.rem(y, 2)
    even_odd = y + 1 - 2 * odd
    odd_even = lax.rem(y + 3 + 2 * odd, 4)
    first, second = (even_odd, odd_even), (odd_even, even_odd)

    def swap(n, src, dst, to):
        return pltpu.make_async_remote_copy(
            src_ref=src, dst_ref=dst, send_sem=swap_send.at[n], recv_sem=swap_recv.at[n],
            device_id=(to, col), device_id_type=MESH,
        )

    swap_all = [swap(h, half_rows(h), known[h].at[pl.ds(32, 32)], first[h]) for h in (0, 1)]
    swap_some = [swap(2 + h, packed[h], got[h], second[h]) for h in (0, 1)]

    pl.semaphore_wait(barrier, 7)
    for copy in swap_all:
        copy.start()

    wide = CHUNKS * WIDE
    chosen = lax.broadcasted_iota(jnp.int32, (512, wide), 0)
    lane_tile = lax.broadcasted_iota(jnp.int32, (512, wide), 1) >> 6
    pick = jnp.where(chosen == lane_tile + col * 16, 1.0, 0.0).astype(jnp.bfloat16)
    int_mask_copy.wait()
    flags = int_mask[...].astype(jnp.float32).astype(jnp.bfloat16)
    flag_rows[...] = jnp.dot(flags, pick, preferred_element_type=jnp.float32)
    ints_copy.wait()

    def mask_chunk(j):
        for t in range(16):
            flag = flag_rows[t : t + 1, j * WIDE : (j + 1) * WIDE]
            spread = jnp.broadcast_to(flag, (TILE, WIDE)).astype(jnp.bfloat16)
            block = ints_in[t * TILE : (t + 1) * TILE, j * WIDE : (j + 1) * WIDE]
            ints_all[j, pl.ds(pl.multiple_of(y * 1024 + t * TILE, TILE), TILE), :] = block * spread

    used = [0]

    def ring(slot, down, up):
        n = used[0]
        used[0] += 1
        return Ring(slot, down, up, ring_send.at[n], ring_recv.at[n])

    def ring_of_chunk(j):
        return ring(
            lambda d, half: ints_all.at[j, pl.ds(pl.multiple_of(turn(y, d) * 1024 + half * 512, 512), 512)],
            down_y, up_y,
        )

    ring_b = [ring_of_chunk(j) for j in range(CHUNKS)]

    mask_chunk(0)
    ring_b[0].start_first()

    for copy in amp_copies:
        copy.wait()
    for h in (0, 1):
        swap_all[h].wait_recv()

        def pack(q, carry, h=h):
            tile = pair_map[second[h] * 32 + q]
            plane, at = tile >> 5, tile & 31
            here = jnp.where(plane == y, at, jnp.where(plane == first[h], at + 32, 0))
            packed[h][q] = known[h][here]
            return carry

        lax.fori_loop(0, 32, pack, 0)
        swap_some[h].start()
    ring_b[0].start_second()
    for j in range(1, CHUNKS):
        mask_chunk(j)
    ring_b[0].forward()
    ring_b[1].start()
    for copy in swap_some:
        copy.wait_recv()

    lane = lax.broadcasted_iota(jnp.int32, (HALF, 128), 1)

    def choose(q, carry):
        tile = pair_map[y * 32 + q]
        plane, at = tile >> 5, tile & 31
        left = amp_mask[lax.rem(col, 4) * 2, tile]
        right = amp_mask[lax.rem(col, 4) * 2 + 1, tile]
        for h in (0, 1):
            mine = jnp.where(plane == y, 1, 0)
            theirs = jnp.where(plane == first[h], 1, 0)
            here = mine + theirs
            there = 1 - here

            def flag(side):
                return jnp.where(lane < TILE, left * side, right * side).astype(jnp.float32).astype(jnp.bfloat16)

            full[col, pl.ds(pl.multiple_of(q * TILE + h * HALF, HALF), HALF), :] = (
                known[h][at + 32 * theirs] * flag(here) + got[h][q] * flag(there)
            )
        return carry

    lax.fori_loop(0, 32, choose, 0)

    relays = {}

    def relay(dx, dz, start, size):
        n = len(relays)
        part = start // 1024
        piece = full.at[place(dx, dz, core), pl.ds(start, size)]
        copy = pltpu.make_async_remote_copy(
            src_ref=piece, dst_ref=piece, send_sem=relay_send.at[n], recv_sem=relay_recv.at[n],
            device_id=twin, device_id_type=MESH,
        )
        copy.start()
        relays[dx, dz, part] = copy

    def rows_of(part, half):
        return pl.ds(part * 1024 + half * 512, 512)

    def ring_x(part, dz):
        return ring(lambda d, half: full.at[place(d, dz, core), rows_of(part, half)], down_x, up_x)

    def ring_z(part, dx):
        return ring(lambda d, half: full.at[place(dx, d, core), rows_of(part, half)], down_z, up_z)

    first_x, first_z = ring_x(0, 0), ring_z(1, 0)
    then_z = {d: ring_z(0, d) for d in (0, -1, 1, 2)}
    then_x = {d: ring_x(1, d) for d in (0, -1, 1, 2)}
    first_x.start()
    first_z.start()
    relay(0, 0, 0, 2048)
    then_z[0].start()
    then_x[0].start()
    def over_rows(body, size, start=0, stop=2048):
        def step(m, carry):
            body(pl.ds(pl.multiple_of(m * size, size), size))
            return carry

        lax.fori_loop(start // size, stop // size, step, 0)

    def quarter(d):
        for share in range(2):
            if share == 0:
                runs = [(pl.multiple_of((zz * 8 + turn(x, d) * 2) * 128, 256), 2) for zz in range(4)]
            else:
                runs = [(pl.multiple_of(turn(z, d) * 1024, 1024), 8)]

            def body(rows):
                left = jnp.concatenate(
                    [full[at // 128 + s, rows, :] for at, n in runs for s in range(n)], axis=1
                )
                for j in range(EARLY):
                    right = jnp.concatenate([ints_all[j, pl.ds(at, n * 128), :] for at, n in runs], axis=0)
                    here = jnp.dot(left, right, preferred_element_type=jnp.float32)
                    if d != 0:
                        here = here + early[j, rows, :]
                    if d != 2:
                        early[j, rows, :] = here
                    else:
                        out[rows, j * WIDE : (j + 1) * WIDE] = here.astype(jnp.bfloat16)

            over_rows(body, PART_STEP, share * 1024, (share + 1) * 1024)

    def relayed(d):
        for e in (0, -1, 1, 2):
            relays[d, e, 0].wait_recv()
            if (e, d) != (0, 0):
                relays[e, d, 1].wait_recv()

    def whole(j, start, stop):
        def body(rows):
            left = jnp.concatenate([full[s, rows, :] for s in range(32)], axis=1)
            out[rows, j * WIDE : (j + 1) * WIDE] = jnp.dot(
                left, ints_all[j], preferred_element_type=jnp.float32
            ).astype(jnp.bfloat16)

        over_rows(body, WHOLE_STEP, start, stop)

    last = CHUNKS - 1

    def part(rows, *planes):
        starts = [turn(y, d) * 8 for d in planes]
        left = jnp.concatenate([full[start + s, rows, :] for start in starts for s in range(8)], axis=1)
        right = jnp.concatenate(
            [ints_all[last, pl.ds(pl.multiple_of(start * 128, 1024), 1024), :] for start in starts], axis=0
        )
        return jnp.dot(left, right, preferred_element_type=jnp.float32)

    def begin(rows):
        total[rows, :] = part(rows, 0)

    def add(rows):
        total[rows, :] += part(rows, -1, 1)

    def end(rows):
        out[rows, last * WIDE : (last + 1) * WIDE] = (total[rows, :] + part(rows, 2)).astype(jnp.bfloat16)

    def near_two(d):
        then_z[d].near()
        then_x[d].near()
        for e in (-1, 1):
            relay(d, e, 0, 1024)
            relay(e, d, 1024, 1024)

    def far_two(d):
        then_z[d].far()
        then_x[d].far()
        relay(d, 2, 0, 1024)
        relay(2, d, 1024, 1024)

    def forward_two(d):
        then_z[d].forward()
        then_x[d].forward()

    def start_two(d):
        then_z[d].start()
        then_x[d].start()

    first_x.forward()
    first_z.forward()
    first_x.near()
    first_z.near()
    start_two(-1)
    for d in (-1, 1):
        relay(d, 0, 0, 1024)
        relay(0, d, 1024, 1024)
    forward_two(0)
    start_two(1)
    near_two(0)
    first_x.far()
    first_z.far()
    relay(2, 0, 0, 1024)
    relay(0, 2, 1024, 1024)
    ring_b[1].forward()
    ring_b[2].start()
    forward_two(-1)
    start_two(2)
    near_two(-1)
    far_two(0)
    for j in range(EARLY):
        ring_b[j].near()
        ring_b[j].far()
    forward_two(1)
    relayed(0)
    quarter(0)
    near_two(1)
    far_two(-1)
    ring_b[2].forward()
    ring_b[3].start()
    relayed(-1)
    quarter(-1)
    forward_two(2)
    near_two(2)
    far_two(1)
    relayed(1)
    quarter(1)
    far_two(2)
    ring_b[2].near()
    ring_b[2].far()
    relayed(2)
    quarter(2)
    whole(2, 0, 1024)
    ring_b[3].forward()
    whole(2, 1024, 2048)
    over_rows(begin, PART_STEP)
    for each in (*ring_b[:3], first_x, first_z, *then_z.values(), *then_x.values()):
        each.finish()
    for copy in (*swap_all, *swap_some, *relays.values()):
        copy.wait_send()
    ring_b[3].near()
    over_rows(add, PART_STEP)
    ring_b[3].far()
    over_rows(end, LAST_STEP)
    ring_b[3].finish()


def write(result, out, sems):
    size = 2048 // WRITES
    copies = [
        pltpu.make_async_copy(result.at[pl.ds(i * size, size)], out.at[pl.ds(i * size, size)], sems.at[i])
        for i in range(WRITES)
    ]
    for copy in copies:
        copy.start()
    for copy in copies:
        copy.wait()


def local(amplitudes, integrals, amp_mask, int_mask, pair_map):
    anywhere = pl.BlockSpec(memory_space=pl.ANY)
    half_tiles = [pltpu.VMEM((n, HALF, 128), jnp.bfloat16) for n in (64, 64, 32, 32, 32, 32)]
    result = pl.pallas_call(
        kernel,
        out_shape=pltpu.VMEM((2048, 1024), jnp.bfloat16),
        in_specs=[anywhere] * 5,
        out_specs=pl.BlockSpec(memory_space=pltpu.VMEM),
        scratch_shapes=[
            pltpu.SMEM((8, 128), jnp.int32),
            pltpu.SMEM((128,), jnp.int32),
            pltpu.VMEM((16, 512), jnp.int32),
            *half_tiles,
            pltpu.VMEM((32, 2048, 128), jnp.bfloat16),
            pltpu.VMEM((1024, 1024), jnp.bfloat16),
            pltpu.VMEM((16, 1024), jnp.float32),
            pltpu.VMEM((CHUNKS, 4096, WIDE), jnp.bfloat16),
            pltpu.VMEM((EARLY, 2048, WIDE), jnp.float32),
            pltpu.VMEM((2048, WIDE), jnp.float32),
            pltpu.SemaphoreType.DMA((RINGS, 6)),
            pltpu.SemaphoreType.DMA((RINGS, 6)),
            pltpu.SemaphoreType.DMA((4,)),
            pltpu.SemaphoreType.DMA((4,)),
            pltpu.SemaphoreType.DMA((RELAYS,)),
            pltpu.SemaphoreType.DMA((RELAYS,)),
            pltpu.SemaphoreType.DMA((6,)),
        ],
        compiler_params=pltpu.CompilerParams(
            collective_id=0, has_side_effects=True, vmem_limit_bytes=52 * 1024 * 1024
        ),
        cost_estimate=pl.CostEstimate(flops=2 * 2048 * 4096 * 1024, bytes_accessed=7 * 2**20, transcendentals=0),
    )(amp_mask.T, pair_map, int_mask, amplitudes.reshape(32, TILE, 128), integrals)
    return pl.pallas_call(
        write,
        out_shape=jax.ShapeDtypeStruct((2048, 1024), jnp.bfloat16),
        in_specs=[pl.BlockSpec(memory_space=pltpu.VMEM)],
        out_specs=anywhere,
        scratch_shapes=[pltpu.SemaphoreType.DMA((WRITES,))],
    )(result)


def solution(mesh):
    in_specs = (P("row", "col"), P("row", "col"), P(), P(), P())
    out_specs = P("row", "col")
    return jax.shard_map(local, mesh=mesh, in_specs=in_specs, out_specs=out_specs, check_vma=False)
```

```python
import jax
import jax.numpy as jnp
from jax import lax
from jax.experimental import pallas as pl
from jax.experimental.pallas import tpu as pltpu
from jax.sharding import PartitionSpec as P

TILE = 64
HALF = TILE // 2
MESH = pl.DeviceIdType.MESH
CHUNKS = 4
EARLY = 2
WIDE = 256
WHOLE_STEP = 512
PART_STEP = 1024
LAST_STEP = 2048
RINGS = CHUNKS + 10
RELAYS = 31


class Ring:
    def __init__(self, slot, down, up, send, recv):
        routes = (
            (slot(0, 0), up),
            (slot(0, 1), down),
            (slot(0, 1), up),
            (slot(0, 0), down),
            (slot(-1, 0), up),
            (slot(1, 1), down),
        )
        self.copies = [
            pltpu.make_async_remote_copy(
                src_ref=piece, dst_ref=piece, send_sem=send.at[i], recv_sem=recv.at[i], device_id=to, device_id_type=MESH
            )
            for i, (piece, to) in enumerate(routes)
        ]

    def start_first(self):
        for copy in self.copies[:2]:
            copy.start()

    def start_second(self):
        for copy in self.copies[2:4]:
            copy.start()

    def start(self):
        self.start_first()
        self.start_second()

    def forward(self):
        for i in (0, 1):
            self.copies[i].wait_recv()
            self.copies[4 + i].start()

    def near(self):
        for copy in self.copies[2:4]:
            copy.wait_recv()

    def far(self):
        for copy in self.copies[4:]:
            copy.wait_recv()

    def finish(self):
        for copy in self.copies:
            copy.wait_send()


def kernel(
    amp_mask_in, pair_map_in, int_mask_in, amp, ints, out,
    amp_mask, pair_map, int_mask, known_0, known_1, packed_0, packed_1, got_0, got_1,
    full, ints_in, flag_rows, ints_all, early, total,
    ring_send, ring_recv, swap_send, swap_recv, relay_send, relay_recv, local_sem,
):
    y = lax.axis_index("row")
    col = lax.axis_index("col")
    core = lax.rem(col, 2)
    x = lax.rem(lax.div(col, 2), 4)
    z = lax.div(col, 8)

    def turn(a, d):
        return lax.rem(a + (d + 4), 4)

    def place(dx, dz, c):
        return turn(z, dz) * 8 + turn(x, dx) * 2 + c

    up_y, down_y = (turn(y, 1), col), (turn(y, -1), col)
    up_x, down_x = (y, place(1, 0, core)), (y, place(-1, 0, core))
    up_z, down_z = (y, place(0, 1, core)), (y, place(0, -1, core))
    twin = (y, place(0, 0, 1 - core))

    barrier = pltpu.get_barrier_semaphore()
    for other in (up_y, down_y, up_x, down_x, up_z, down_z, twin):
        pl.semaphore_signal(barrier, inc=1, device_id=other, device_id_type=MESH)

    known, packed, got = (known_0, known_1), (packed_0, packed_1), (got_0, got_1)

    def half_rows(h):
        return amp.at[:, pl.ds(h * HALF, HALF)]

    mask_row = pl.multiple_of(lax.div(col, 4) * 8, 8)
    own_row = pl.multiple_of(y * 16, 16)
    ints_copy = pltpu.make_async_copy(ints, ints_in, local_sem.at[0])
    int_mask_copy = pltpu.make_async_copy(int_mask_in.at[pl.ds(own_row, 16)], int_mask, local_sem.at[1])
    amp_copies = [
        pltpu.make_async_copy(amp_mask_in.at[pl.ds(mask_row, 8)], amp_mask, local_sem.at[2]),
        pltpu.make_async_copy(pair_map_in, pair_map, local_sem.at[3]),
        pltpu.make_async_copy(half_rows(0), known_0.at[pl.ds(0, 32)], local_sem.at[4]),
        pltpu.make_async_copy(half_rows(1), known_1.at[pl.ds(0, 32)], local_sem.at[5]),
    ]
    for copy in (*amp_copies[2:], int_mask_copy, ints_copy, *amp_copies[:2]):
        copy.start()

    odd = lax.rem(y, 2)
    even_odd = y + 1 - 2 * odd
    odd_even = lax.rem(y + 3 + 2 * odd, 4)
    first, second = (even_odd, odd_even), (odd_even, even_odd)

    def swap(n, src, dst, to):
        return pltpu.make_async_remote_copy(
            src_ref=src, dst_ref=dst, send_sem=swap_send.at[n], recv_sem=swap_recv.at[n],
            device_id=(to, col), device_id_type=MESH,
        )

    swap_all = [swap(h, known[h].at[pl.ds(0, 32)], known[h].at[pl.ds(32, 32)], first[h]) for h in (0, 1)]
    swap_some = [swap(2 + h, packed[h], got[h], second[h]) for h in (0, 1)]

    pl.semaphore_wait(barrier, 7)
    for h in (0, 1):
        amp_copies[2 + h].wait()
        swap_all[h].start()

    wide = CHUNKS * WIDE
    chosen = lax.broadcasted_iota(jnp.int32, (512, wide), 0)
    lane_tile = lax.broadcasted_iota(jnp.int32, (512, wide), 1) >> 6
    pick = jnp.where(chosen == lane_tile + col * 16, 1.0, 0.0).astype(jnp.bfloat16)
    int_mask_copy.wait()
    flags = int_mask[...].astype(jnp.float32).astype(jnp.bfloat16)
    flag_rows[...] = jnp.dot(flags, pick, preferred_element_type=jnp.float32)
    ints_copy.wait()

    def mask_chunk(j):
        for t in range(16):
            flag = flag_rows[t : t + 1, j * WIDE : (j + 1) * WIDE]
            spread = jnp.broadcast_to(flag, (TILE, WIDE)).astype(jnp.bfloat16)
            block = ints_in[t * TILE : (t + 1) * TILE, j * WIDE : (j + 1) * WIDE]
            ints_all[j, pl.ds(pl.multiple_of(y * 1024 + t * TILE, TILE), TILE), :] = block * spread

    used = [0]

    def ring(slot, down, up):
        n = used[0]
        used[0] += 1
        return Ring(slot, down, up, ring_send.at[n], ring_recv.at[n])

    def ring_of_chunk(j):
        return ring(
            lambda d, half: ints_all.at[j, pl.ds(pl.multiple_of(turn(y, d) * 1024 + half * 512, 512), 512)],
            down_y, up_y,
        )

    ring_b = [ring_of_chunk(j) for j in range(CHUNKS)]

    mask_chunk(0)
    ring_b[0].start_first()

    for copy in amp_copies[:2]:
        copy.wait()
    for h in (0, 1):
        swap_all[h].wait_recv()

        def pack(q, carry, h=h):
            tile = pair_map[second[h] * 32 + q]
            plane, at = tile >> 5, tile & 31
            here = jnp.where(plane == y, at, jnp.where(plane == first[h], at + 32, 0))
            packed[h][q] = known[h][here]
            return carry

        lax.fori_loop(0, 32, pack, 0)
        swap_some[h].start()
    ring_b[0].start_second()
    for j in range(1, CHUNKS):
        mask_chunk(j)
    ring_b[0].forward()
    ring_b[1].start()
    for copy in swap_some:
        copy.wait_recv()

    lane = lax.broadcasted_iota(jnp.int32, (HALF, 128), 1)

    def choose(q, carry):
        tile = pair_map[y * 32 + q]
        plane, at = tile >> 5, tile & 31
        left = amp_mask[lax.rem(col, 4) * 2, tile]
        right = amp_mask[lax.rem(col, 4) * 2 + 1, tile]
        for h in (0, 1):
            mine = jnp.where(plane == y, 1, 0)
            theirs = jnp.where(plane == first[h], 1, 0)
            here = mine + theirs
            there = 1 - here

            def flag(side):
                return jnp.where(lane < TILE, left * side, right * side).astype(jnp.float32).astype(jnp.bfloat16)

            full[col, pl.ds(pl.multiple_of(q * TILE + h * HALF, HALF), HALF), :] = (
                known[h][at + 32 * theirs] * flag(here) + got[h][q] * flag(there)
            )
        return carry

    lax.fori_loop(0, 32, choose, 0)

    relays = {}

    def relay(dx, dz, start, size):
        n = len(relays)
        part = start // 1024
        piece = full.at[place(dx, dz, core), pl.ds(start, size)]
        copy = pltpu.make_async_remote_copy(
            src_ref=piece, dst_ref=piece, send_sem=relay_send.at[n], recv_sem=relay_recv.at[n],
            device_id=twin, device_id_type=MESH,
        )
        copy.start()
        relays[dx, dz, part] = copy

    def rows_of(part, half):
        return pl.ds(part * 1024 + half * 512, 512)

    def ring_x(part, dz):
        return ring(lambda d, half: full.at[place(d, dz, core), rows_of(part, half)], down_x, up_x)

    def ring_z(part, dx):
        return ring(lambda d, half: full.at[place(dx, d, core), rows_of(part, half)], down_z, up_z)

    first_x, first_z = ring_x(0, 0), ring_z(1, 0)
    then_z = {d: ring_z(0, d) for d in (0, -1, 1, 2)}
    then_x = {d: ring_x(1, d) for d in (0, -1, 1, 2)}
    first_x.start()
    first_z.start()
    relay(0, 0, 0, 2048)
    then_z[0].start()
    then_x[0].start()
    def over_rows(body, size, start=0, stop=2048):
        def step(m, carry):
            body(pl.ds(pl.multiple_of(m * size, size), size))
            return carry

        lax.fori_loop(start // size, stop // size, step, 0)

    def quarter(d):
        for share in range(2):
            if share == 0:
                runs = [(pl.multiple_of((zz * 8 + turn(x, d) * 2) * 128, 256), 2) for zz in range(4)]
            else:
                runs = [(pl.multiple_of(turn(z, d) * 1024, 1024), 8)]

            def body(rows):
                left = jnp.concatenate(
                    [full[at // 128 + s, rows, :] for at, n in runs for s in range(n)], axis=1
                )
                for j in range(EARLY):
                    right = jnp.concatenate([ints_all[j, pl.ds(at, n * 128), :] for at, n in runs], axis=0)
                    here = jnp.dot(left, right, preferred_element_type=jnp.float32)
                    if d != 0:
                        here = here + early[j, rows, :]
                    if d != 2:
                        early[j, rows, :] = here
                    else:
                        out[rows, j * WIDE : (j + 1) * WIDE] = here.astype(jnp.bfloat16)

            over_rows(body, PART_STEP, share * 1024, (share + 1) * 1024)

    def relayed(d):
        for e in (0, -1, 1, 2):
            relays[d, e, 0].wait_recv()
            if (e, d) != (0, 0):
                relays[e, d, 1].wait_recv()

    def whole(j, start, stop):
        def body(rows):
            left = jnp.concatenate([full[s, rows, :] for s in range(32)], axis=1)
            out[rows, j * WIDE : (j + 1) * WIDE] = jnp.dot(
                left, ints_all[j], preferred_element_type=jnp.float32
            ).astype(jnp.bfloat16)

        over_rows(body, WHOLE_STEP, start, stop)

    last = CHUNKS - 1

    def part(rows, *planes):
        starts = [turn(y, d) * 8 for d in planes]
        left = jnp.concatenate([full[start + s, rows, :] for start in starts for s in range(8)], axis=1)
        right = jnp.concatenate(
            [ints_all[last, pl.ds(pl.multiple_of(start * 128, 1024), 1024), :] for start in starts], axis=0
        )
        return jnp.dot(left, right, preferred_element_type=jnp.float32)

    def begin(rows):
        total[rows, :] = part(rows, 0)

    def add(rows):
        total[rows, :] += part(rows, -1, 1)

    def end(rows):
        out[rows, last * WIDE : (last + 1) * WIDE] = (total[rows, :] + part(rows, 2)).astype(jnp.bfloat16)

    def near_two(d):
        then_z[d].near()
        then_x[d].near()
        for e in (-1, 1):
            relay(d, e, 0, 1024)
            relay(e, d, 1024, 1024)

    def far_two(d):
        then_z[d].far()
        then_x[d].far()
        relay(d, 2, 0, 1024)
        relay(2, d, 1024, 1024)

    def forward_two(d):
        then_z[d].forward()
        then_x[d].forward()

    def start_two(d):
        then_z[d].start()
        then_x[d].start()

    first_x.forward()
    first_z.forward()
    first_x.near()
    first_z.near()
    start_two(-1)
    for d in (-1, 1):
        relay(d, 0, 0, 1024)
        relay(0, d, 1024, 1024)
    forward_two(0)
    start_two(1)
    near_two(0)
    first_x.far()
    first_z.far()
    relay(2, 0, 0, 1024)
    relay(0, 2, 1024, 1024)
    ring_b[1].forward()
    ring_b[2].start()
    forward_two(-1)
    start_two(2)
    near_two(-1)
    far_two(0)
    for j in range(EARLY):
        ring_b[j].near()
        ring_b[j].far()
    forward_two(1)
    relayed(0)
    quarter(0)
    near_two(1)
    far_two(-1)
    ring_b[2].forward()
    ring_b[3].start()
    relayed(-1)
    quarter(-1)
    forward_two(2)
    near_two(2)
    far_two(1)
    relayed(1)
    quarter(1)
    far_two(2)
    ring_b[2].near()
    ring_b[2].far()
    relayed(2)
    quarter(2)
    whole(2, 0, 1024)
    ring_b[3].forward()
    whole(2, 1024, 2048)
    over_rows(begin, PART_STEP)
    for each in (*ring_b[:3], first_x, first_z, *then_z.values(), *then_x.values()):
        each.finish()
    for copy in (*swap_all, *swap_some, *relays.values()):
        copy.wait_send()
    ring_b[3].near()
    over_rows(add, PART_STEP)
    ring_b[3].far()
    over_rows(end, LAST_STEP)
    ring_b[3].finish()


def local(amplitudes, integrals, amp_mask, int_mask, pair_map):
    anywhere = pl.BlockSpec(memory_space=pl.ANY)
    half_tiles = [pltpu.VMEM((n, HALF, 128), jnp.bfloat16) for n in (64, 64, 32, 32, 32, 32)]
    return pl.pallas_call(
        kernel,
        out_shape=pltpu.VMEM((2048, 1024), jnp.bfloat16),
        in_specs=[anywhere] * 5,
        out_specs=pl.BlockSpec(memory_space=pltpu.VMEM),
        scratch_shapes=[
            pltpu.SMEM((8, 128), jnp.int32),
            pltpu.SMEM((128,), jnp.int32),
            pltpu.VMEM((16, 512), jnp.int32),
            *half_tiles,
            pltpu.VMEM((32, 2048, 128), jnp.bfloat16),
            pltpu.VMEM((1024, 1024), jnp.bfloat16),
            pltpu.VMEM((16, 1024), jnp.float32),
            pltpu.VMEM((CHUNKS, 4096, WIDE), jnp.bfloat16),
            pltpu.VMEM((EARLY, 2048, WIDE), jnp.float32),
            pltpu.VMEM((2048, WIDE), jnp.float32),
            pltpu.SemaphoreType.DMA((RINGS, 6)),
            pltpu.SemaphoreType.DMA((RINGS, 6)),
            pltpu.SemaphoreType.DMA((4,)),
            pltpu.SemaphoreType.DMA((4,)),
            pltpu.SemaphoreType.DMA((RELAYS,)),
            pltpu.SemaphoreType.DMA((RELAYS,)),
            pltpu.SemaphoreType.DMA((6,)),
        ],
        compiler_params=pltpu.CompilerParams(
            collective_id=0, has_side_effects=True, vmem_limit_bytes=52 * 1024 * 1024
        ),
        cost_estimate=pl.CostEstimate(flops=2 * 2048 * 4096 * 1024, bytes_accessed=7 * 2**20, transcendentals=0),
    )(amp_mask.T, pair_map, int_mask, amplitudes.reshape(32, TILE, 128), integrals)


def solution(mesh):
    in_specs = (P("row", "col"), P("row", "col"), P(), P(), P())
    out_specs = P("row", "col")
    return jax.shard_map(local, mesh=mesh, in_specs=in_specs, out_specs=out_specs, check_vma=False)
```
